256 devices in a mesh: orient: 64 (over x_lo, y, z), zslab: 4 (over x_hi, core).
Axes of the slice: x: 4 (x_hi: 2, x_lo: 2; x = x_hi * 2 + x_lo), y: 4, z: 8, core: 2. Of those that a mesh axis runs over, the one named last changes fastest.
Arguments:
- volume: float32 [32, 256, 256], P('zslab'), may hold values from -60 to 60, as said below
- templates: float32 [64, 16, 16, 16], P('orient'), may hold values from -6 to 6
- wedge: int32 [16, 16, 16], replicated, may hold values 0 or 1
Outputs:
- best: float32 [32, 256, 256], P('zslab', 'orient')
The draws below stay inside these ranges and needn't reach their ends.
Inputs may be any that keep to these rules, and one draw needn't show every extreme that they name: `volume`: A tomogram whose contrast varies between z layers and between x planes.
All inputs are finite; a program needn't handle non-finite values.
Results may differ from the reference program's by a relative error of at most 0.0001.
Values sent between devices are 32-bit elements; how exact they have to be, the bound alone decides.
No kernel may reach another device: no remote copies, remote signals or barrier semaphores. Data moves between devices by JAX's collectives and lax.ppermute only.
A program may use at most 128 MiB of HBM per device.

```python
import jax
import jax.numpy as jnp
from jax import lax

TS = 16
NX = 256
NY = 256
NZ = 32
ORIENTS = 64


def draw_volume(key, part):
    key = jax.random.fold_in(key, 7)
    first, second, third = jax.random.split(key, 3)
    layer_scale = jnp.exp(jax.random.uniform(second, (NZ, 1, 1), jnp.float32) * 1.1513)
    plane_scale = jnp.exp(jax.random.uniform(third, (1, NX, 1), jnp.float32) * 1.1513)
    base = jnp.clip(jax.random.normal(first, (NZ, NX, NY), jnp.float32), -6.0, 6.0)
    return base * layer_scale * plane_scale


def set_ends(result, stream_key, low, largest):
    shape = result.shape
    index_at = [jax.random.randint(jax.random.fold_in(stream_key, axis), (), 0, shape[axis]) for axis in range(len(shape))]
    result = result.at[tuple(index_at)].set(low)
    longest = shape.index(max(shape))
    index_at[longest] = (index_at[longest] + 1) % shape[longest]
    return result.at[tuple(index_at)].set(largest)


def block_levels(own_key, dims, cuts, least, top_value):
    gain, own = 1.0, jax.random.fold_in(own_key, 6)
    for position, blocks in cuts:
        heights = jnp.exp(jax.random.uniform(jax.random.fold_in(own, position), (blocks,), jnp.float32, least / len(cuts), top_value / len(cuts)))
        gain = gain * jnp.repeat(heights, dims[position] // blocks).reshape([-1 if axis == position else 1 for axis in range(len(dims))])
    return gain


def normal_values(rng, shape, width, reach, pieces=(), kind=jnp.bfloat16):
    values = jax.random.normal(rng, shape, jnp.float32) * width
    if len(pieces) > 0:
        values = block_levels(rng, shape, pieces, -0.22, 0.18) * values
    return jnp.clip(values, min=-reach, max=reach).astype(kind)


def setup_inputs(seed: int = 0) -> dict:
    splits = jax.random.split(jax.random.key(seed), 4)
    return {
        "volume": draw_volume(jax.random.fold_in(splits[3], 71), 0),
        "templates": normal_values(splits[1], (ORIENTS, TS, TS, TS), 1.0, 6.0, ((0, 64),), jnp.float32),
        "wedge": set_ends((jax.random.randint(splits[2], (TS, TS, TS), 0, 3) < 2).astype(jnp.int32), jax.random.fold_in(splits[2], 1), 0, 1),
    }


def filter_template(template, wedge):
    spec = jnp.fft.fftn(template)
    filt = jnp.real(jnp.fft.ifftn(spec * wedge.astype(jnp.float32))).astype(jnp.float32)
    centered = filt - jnp.mean(filt)
    return centered / jnp.sqrt(jnp.sum(centered * centered) + 1e-05)

def reference(volume, templates, wedge):
    half = TS // 2
    padded = jnp.pad(volume, ((half, half), (0, 0), (0, 0)))
    vol_spec = jnp.fft.fftn(padded)
    squared = padded * padded
    energy = jnp.zeros((NZ, NX, NY), jnp.float32)
    for layer in range(TS):
        energy = energy + squared[layer:layer + NZ]
    summed = jnp.zeros_like(energy)
    for shift in range(TS):
        summed = summed + jnp.roll(energy, half - shift, axis=1)
    energy = jnp.zeros_like(summed)
    for shift in range(TS):
        energy = energy + jnp.roll(summed, half - shift, axis=2)
    scale = 1.0 / jnp.sqrt(energy / float(TS ** 3) + 1e-05)

    def one(carry, template):
        normed = filter_template(template, wedge)
        grid = jnp.zeros((NZ + TS, NX, NY), jnp.float32).at[:TS, :TS, :TS].set(normed)
        grid = jnp.roll(grid, (-half, -half, -half), axis=(0, 1, 2))
        corr = jnp.real(jnp.fft.ifftn(jnp.conj(jnp.fft.fftn(grid)) * vol_spec)).astype(jnp.float32)
        score = corr[half:half + NZ] * scale
        return (jnp.maximum(carry, score), None)
    start = jnp.full((NZ, NX, NY), -jnp.inf, jnp.float32)
    best, unused = lax.scan(one, start, templates)
    return best
```

```python
import math

import jax
import jax.numpy as jnp
import numpy as np
from jax import lax
from jax.experimental import pallas as pl
from jax.experimental.pallas import tpu as pltpu
from jax.sharding import PartitionSpec as P

TS = 16
HALF = 8
NF = 32
NK = 16
SLAB = 8
NY = 256
GROUP = 4
NO = 16
STRIP = 4
LANES = 128
KDIM = TS * 48
EXACT = lax.Precision.HIGHEST
VMEM = pl.BlockSpec(memory_space=pltpu.VMEM)
SMEM = pl.BlockSpec(memory_space=pltpu.SMEM)


def plus(a, b):
    if a is None:
        return b
    return a if b is None else a + b


def minus(a, b):
    if b is None:
        return a
    return -b if a is None else a - b


def twiddled(value, k, count, sign):
    re, im = value
    if k == 0:
        return value
    if 4 * k == count:
        return (None if im is None else -sign * im, None if re is None else sign * re)
    c = math.cos(2.0 * math.pi * k / count)
    s = sign * math.sin(2.0 * math.pi * k / count)
    if im is None:
        return (c * re, s * re)
    if re is None:
        return (-s * im, c * im)
    return (c * re - s * im, s * re + c * im)


def forward(rows):
    count = len(rows)
    if count == 2:
        return [(plus(rows[0], rows[1]), None), (minus(rows[0], rows[1]), None)]
    even, odd = forward(rows[::2]), forward(rows[1::2])
    bins = [None] * (count // 2 + 1)
    for k in range(count // 4 + 1):
        e, o = even[k], twiddled(odd[k], k, count, -1.0)
        bins[k] = (plus(e[0], o[0]), plus(e[1], o[1]))
        if 4 * k != count:
            re, im = minus(e[0], o[0]), minus(e[1], o[1])
            bins[count // 2 - k] = (re, None if im is None else -im)
    return bins


def inverse(bins, count, need):
    if count == 2:
        first = bins[0][0] + bins[1][0]
        return [first] if need == 1 else [first, bins[0][0] - bins[1][0]]
    even, odd = [], []
    for k in range(count // 4 + 1):
        a, b = bins[k], bins[count // 2 - k]
        if k == 0:
            even.append((a[0] + b[0], None))
            odd.append((a[0] - b[0], None))
        elif 4 * k == count:
            even.append((2.0 * a[0], None))
            odd.append((-2.0 * a[1], None))
        else:
            even.append((a[0] + b[0], a[1] - b[1]))
            odd.append(twiddled((a[0] - b[0], a[1] + b[1]), k, count, 1.0))
    evens = inverse(even, count // 2, (need + 1) // 2)
    odds = inverse(odd, count // 2, need // 2)
    rows = [None] * need
    rows[::2] = evens
    rows[1::2] = odds
    return rows


def slots(bins):
    return [(bins[0][0], bins[NK][0])] + [bins[k] for k in range(1, NK)]


def unslot(pairs):
    return [(pairs[0][0], None)] + list(pairs[1:]) + [(pairs[0][1], None)]


def halves(value):
    high = value.astype(jnp.bfloat16)
    return high, (value - high.astype(jnp.float32)).astype(jnp.bfloat16)


def filter_tables():
    small = np.arange(TS)
    pair = 2.0 * math.pi * np.outer(small, small) / TS
    two = pair[:, None, :, None] + pair[None, :, None, :]
    two = two.reshape(TS * TS, TS * TS)
    right = np.concatenate([np.cos(two), -np.sin(two)], axis=1)
    c, s = np.cos(pair), np.sin(pair)
    ahead = np.block([[c, s], [-s, c]])
    back = np.block([[c, -s], [s, c]])
    return tuple(np.asarray(t, np.float32) for t in (right, ahead, back))


def spread_table():
    out = np.zeros((TS, TS, TS, 48), np.float32)
    for b in range(TS):
        for c in range(TS):
            out[b, c, b, c] = 1.0
    return out.reshape(TS * TS, KDIM)


def filter_kernel(template_ref, wedge_ref, right_ref, ahead_ref, back_ref, out_ref):
    def product(a, b):
        return jnp.dot(a, b, precision=EXACT, preferred_element_type=jnp.float32)

    width = TS * TS
    spec = product(template_ref[...], right_ref[...])
    spec = jnp.concatenate([spec[:, :width], spec[:, width:]], axis=0)
    keep = wedge_ref[...]
    spec = product(ahead_ref[...], spec) * jnp.concatenate([keep, keep], axis=0)
    spec = product(back_ref[...], spec)
    filt = product(spec[:TS], right_ref[:, :width]) + product(spec[TS:], right_ref[:, width:])
    filt = filt * (1.0 / float(TS**3))
    centered = filt - jnp.sum(filt) * (1.0 / float(TS**3))
    out_ref[...] = centered / jnp.sqrt(jnp.sum(centered * centered) + 1e-05)


def volume_kernel(place_ref, lower_ref, own_ref, upper_ref, high_ref, low_ref, scale_ref, spec_ref):
    for block, ref in enumerate((lower_ref, own_ref, upper_ref)):
        for lane in range(0, NY, LANES):
            bins = forward([ref[x, :, lane : lane + LANES] for x in range(NF)])
            for k, (re, im) in enumerate(slots(bins)):
                spec_ref[k, 8 * block : 8 * block + 8, lane : lane + LANES] = re
                spec_ref[k, 24 + 8 * block : 32 + 8 * block, lane : lane + LANES] = im

    def split(k, carry):
        high_ref[k], low_ref[k] = halves(spec_ref[k])
        return carry

    lax.fori_loop(0, NK, split, 0)
    first = place_ref[0] * STRIP
    sums = []
    for x in range(STRIP + TS - 1):
        layers = jnp.concatenate([r[first + x] for r in (lower_ref, own_ref, upper_ref)], axis=0)
        sums.append(layers * layers)
    for step in (1, 2, 4, 8):
        sums = [sums[i] + sums[i + step] for i in range(len(sums) - step)]
    for x in range(STRIP):
        total = sums[x]
        for step in (1, 2, 4, 8):
            total = total + pltpu.roll(total, 24 - step, axis=0)
        total = total[:SLAB]
        for step in (1, 2, 4, 8):
            total = total + pltpu.roll(total, NY - step, axis=1)
        total = pltpu.roll(total, HALF, axis=1)
        scale_ref[x] = (1.0 / NF) / jnp.sqrt(total * (1.0 / float(TS**3)) + 1e-05)


def score_kernel(
    place_ref, a_ref, b_ref, c_ref, d_ref, spread_ref, high_ref, low_ref,
    out0_ref, out1_ref, out2_ref, out3_ref,
    wide_ref, base_ref, base_high, base_low, left_ref, right_high, right_low, prod_ref, best_ref,
):
    for quarter, ref in enumerate((a_ref, b_ref, c_ref, d_ref)):
        high, low = halves(ref[...])
        rows = ref.shape[0]
        wide = jnp.dot(
            high, spread_ref[...], preferred_element_type=jnp.float32
        ) + jnp.dot(low, spread_ref[...], preferred_element_type=jnp.float32)
        for j in range(KDIM // LANES):
            wide_ref[j, rows * quarter : rows * quarter + rows, :] = wide[:, j * LANES : (j + 1) * LANES]
    for o in range(0, NO, 8):
        for lane in range(0, KDIM, LANES):
            rows = [
                wide_ref[lane // LANES, pl.ds(o * TS + a, 8, stride=TS), :] for a in range(TS)
            ]
            bins = forward(rows + [None] * (NF - TS))
            for k, (re, im) in enumerate(slots(bins)):
                base_ref[k, 0, o : o + 8, lane : lane + LANES] = re
                base_ref[k, 1, o : o + 8, lane : lane + LANES] = im

    def assemble(k, carry):
        re, im = base_ref[k, 0], base_ref[k, 1]
        packed = (k == 0).astype(jnp.float32)
        mixed = 1.0 - packed
        first = re + mixed * pltpu.roll(im, 24, axis=1)
        second = pltpu.roll(mixed * re + packed * im, 24, axis=1) - mixed * im
        base_high[k, 0], base_low[k, 0] = halves(first)
        base_high[k, 1], base_low[k, 1] = halves(second)
        return carry

    lax.fori_loop(0, NK, assemble, 0)

    def one(k, carry):
        for part in range(2):
            for row0, ref in ((0, base_high), (256, base_low)):
                value = ref[k, part]
                for z in range(SLAB):
                    at = row0 + part * 128 + z * NO
                    left_ref[at : at + NO, :] = value if z == 0 else pltpu.roll(value, z, axis=1)
        for src, dst in ((high_ref, right_high), (low_ref, right_low)):
            value = src[k]
            for b in range(TS):
                shift = (HALF - b) % NY
                dst[48 * b : 48 * b + 48, :] = value if shift == 0 else pltpu.roll(value, shift, axis=1)
        both = jnp.dot(left_ref[...], right_high[...], preferred_element_type=jnp.float32)
        low = jnp.dot(left_ref[:256], right_low[...], preferred_element_type=jnp.float32)
        prod_ref[k] = both[:256] + (both[256:] + low)
        return carry

    lax.fori_loop(0, NK, one, 0)

    best_ref[...] = jnp.zeros_like(best_ref)

    def finish(z, carry):
        row = pl.multiple_of(z * NO, NO)
        here = lax.broadcasted_iota(jnp.int32, (SLAB, LANES), 0) == z
        for lane in range(0, NY, LANES):
            top = None
            for o in (0, 8):
                pairs = [
                    (
                        prod_ref[k, pl.ds(row + o, 8), lane : lane + LANES],
                        prod_ref[k, pl.ds(128 + row + o, 8), lane : lane + LANES],
                    )
                    for k in range(NK)
                ]
                rows = inverse(unslot(pairs), NF, NF // 2)
                top = rows if top is None else [jnp.maximum(a, b) for a, b in zip(top, rows)]
            for x in range(NF // 2):
                largest = jnp.max(top[x], axis=0, keepdims=True)
                best_ref[x, :, lane : lane + LANES] = jnp.where(
                    here, largest, best_ref[x, :, lane : lane + LANES]
                )
        return carry

    lax.fori_loop(0, SLAB, finish, 0)
    mine = place_ref[0]
    for m, ref in enumerate((out0_ref, out1_ref, out2_ref, out3_ref)):
        ref[...] = best_ref[pl.ds((mine ^ m) * STRIP, STRIP)]


def last_kernel(scale_ref, a_ref, b_ref, c_ref, d_ref, out_ref):
    for x in range(STRIP):
        top = jnp.maximum(jnp.maximum(a_ref[x], b_ref[x]), jnp.maximum(c_ref[x], d_ref[x]))
        out_ref[:, x, :] = top * scale_ref[x]


def call(kernel, outs, scratch, args, specs, flops=0, nbytes=0):
    return pl.pallas_call(
        kernel,
        out_shape=outs,
        in_specs=specs,
        out_specs=[VMEM] * len(outs) if isinstance(outs, (list, tuple)) else VMEM,
        scratch_shapes=scratch,
        compiler_params=pltpu.CompilerParams(vmem_limit_bytes=48 * 1024 * 1024),
        cost_estimate=pl.CostEstimate(flops=flops, bytes_accessed=nbytes, transcendentals=0),
    )(*args)


def shards(volume, templates, wedge):
    f32, bf16 = jnp.float32, jnp.bfloat16
    count = lax.axis_size("orient")
    me = lax.axis_index("orient")
    place = (me % GROUP).astype(jnp.int32).reshape(1)
    region = me // GROUP

    def swap(value, mask):
        return lax.ppermute(value, "orient", [(i, i ^ mask) for i in range(count)])

    template = jnp.transpose(templates[0], (1, 2, 0)).reshape(TS, TS * TS)
    keep = jnp.transpose(wedge.astype(f32), (1, 2, 0)).reshape(TS, TS * TS)
    normed = call(
        filter_kernel, jax.ShapeDtypeStruct((TS, TS * TS), f32), [],
        (template, keep) + filter_tables(), [VMEM] * 5, 1 << 22, 1 << 20,
    )
    four = jnp.concatenate([normed] + [swap(normed, m) for m in (4, 16, 20)], axis=0)
    gathered = [four] + [swap(four, m) for m in (8, 32, 40)]

    rows = volume.shape[1]
    pieces = [
        lax.dynamic_slice_in_dim(volume, (region * 16 - HALF + 8 * j) % rows, 8, 1) for j in range(4)
    ]
    window = jnp.transpose(jnp.concatenate(pieces, axis=1), (1, 0, 2))
    slabs = lax.axis_size("zslab")
    lower = lax.ppermute(window, "zslab", [(s, s + 1) for s in range(slabs - 1)])
    upper = lax.ppermute(window, "zslab", [(s + 1, s) for s in range(slabs - 1)])
    high, low, scale = call(
        volume_kernel,
        (
            jax.ShapeDtypeStruct((NK, 48, NY), bf16),
            jax.ShapeDtypeStruct((NK, 48, NY), bf16),
            jax.ShapeDtypeStruct((STRIP, SLAB, NY), f32),
        ),
        [pltpu.VMEM((NK, 48, NY), f32)],
        (place, lower, window, upper), [SMEM] + [VMEM] * 3, 1 << 24, 1 << 21,
    )
    spread = jnp.asarray(spread_table(), bf16)
    strip = jax.ShapeDtypeStruct((STRIP, SLAB, NY), f32)
    parts = call(
        score_kernel, (strip,) * 4,
        [
            pltpu.VMEM((KDIM // LANES, NO * TS, LANES), f32),
            pltpu.VMEM((NK, 2, NO, KDIM), f32),
            pltpu.VMEM((NK, 2, NO, KDIM), bf16),
            pltpu.VMEM((NK, 2, NO, KDIM), bf16),
            pltpu.VMEM((512, KDIM), bf16),
            pltpu.VMEM((KDIM, NY), bf16),
            pltpu.VMEM((KDIM, NY), bf16),
            pltpu.VMEM((NK, 256, NY), f32),
            pltpu.VMEM((NF // 2, SLAB, NY), f32),
        ],
        (place, *gathered, spread, high, low), [SMEM] + [VMEM] * 7, 1 << 33, 1 << 21,
    )
    arrived = [parts[0]] + [swap(parts[m], m) for m in range(1, GROUP)]
    return call(
        last_kernel, jax.ShapeDtypeStruct((SLAB, STRIP, NY), f32), [],
        (scale, *arrived), [VMEM] * 5, 1 << 16, 1 << 18,
    )


def solution(mesh):
    return jax.shard_map(
        shards,
        mesh=mesh,
        in_specs=(P("zslab", None, None), P("orient", None, None, None), P()),
        out_specs=P("zslab", "orient", None),
        check_vma=False,
    )
```

```python
import math

import jax
import jax.numpy as jnp
import numpy as np
from jax import lax
from jax.experimental import pallas as pl
from jax.experimental.pallas import tpu as pltpu
from jax.sharding import PartitionSpec as P

TS = 16
HALF = 8
NF = 32
NK = 16
SLAB = 8
NY = 256
GROUP = 4
NO = 16
STRIP = 4
LANES = 128
KDIM = TS * 48
EXACT = lax.Precision.HIGHEST
VMEM = pl.BlockSpec(memory_space=pltpu.VMEM)
SMEM = pl.BlockSpec(memory_space=pltpu.SMEM)


def plus(a, b):
    if a is None:
        return b
    return a if b is None else a + b


def minus(a, b):
    if b is None:
        return a
    return -b if a is None else a - b


def twiddled(value, k, count, sign):
    re, im = value
    if k == 0:
        return value
    if 4 * k == count:
        return (None if im is None else -sign * im, None if re is None else sign * re)
    c = math.cos(2.0 * math.pi * k / count)
    s = sign * math.sin(2.0 * math.pi * k / count)
    if im is None:
        return (c * re, s * re)
    if re is None:
        return (-s * im, c * im)
    return (c * re - s * im, s * re + c * im)


def forward(rows):
    count = len(rows)
    if count == 2:
        return [(plus(rows[0], rows[1]), None), (minus(rows[0], rows[1]), None)]
    even, odd = forward(rows[::2]), forward(rows[1::2])
    bins = [None] * (count // 2 + 1)
    for k in range(count // 4 + 1):
        e, o = even[k], twiddled(odd[k], k, count, -1.0)
        bins[k] = (plus(e[0], o[0]), plus(e[1], o[1]))
        if 4 * k != count:
            re, im = minus(e[0], o[0]), minus(e[1], o[1])
            bins[count // 2 - k] = (re, None if im is None else -im)
    return bins


def inverse(bins, count, need):
    if count == 2:
        first = bins[0][0] + bins[1][0]
        return [first] if need == 1 else [first, bins[0][0] - bins[1][0]]
    even, odd = [], []
    for k in range(count // 4 + 1):
        a, b = bins[k], bins[count // 2 - k]
        if k == 0:
            even.append((a[0] + b[0], None))
            odd.append((a[0] - b[0], None))
        elif 4 * k == count:
            even.append((2.0 * a[0], None))
            odd.append((-2.0 * a[1], None))
        else:
            even.append((a[0] + b[0], a[1] - b[1]))
            odd.append(twiddled((a[0] - b[0], a[1] + b[1]), k, count, 1.0))
    evens = inverse(even, count // 2, (need + 1) // 2)
    odds = inverse(odd, count // 2, need // 2)
    rows = [None] * need
    rows[::2] = evens
    rows[1::2] = odds
    return rows


def slots(bins):
    return [(bins[0][0], bins[NK][0])] + [bins[k] for k in range(1, NK)]


def unslot(pairs):
    return [(pairs[0][0], None)] + list(pairs[1:]) + [(pairs[0][1], None)]


def halves(value):
    high = value.astype(jnp.bfloat16)
    return high, (value - high.astype(jnp.float32)).astype(jnp.bfloat16)


def filter_tables():
    small = np.arange(TS)
    pair = 2.0 * math.pi * np.outer(small, small) / TS
    two = pair[:, None, :, None] + pair[None, :, None, :]
    two = two.reshape(TS * TS, TS * TS)
    right = np.concatenate([np.cos(two), -np.sin(two)], axis=1)
    c, s = np.cos(pair), np.sin(pair)
    ahead = np.block([[c, s], [-s, c]])
    back = np.block([[c, -s], [s, c]])
    return tuple(np.asarray(t, np.float32) for t in (right, ahead, back))


def spread_table():
    out = np.zeros((2, TS, TS, TS, 48), np.float32)
    for part in range(2):
        for b in range(TS):
            for c in range(TS):
                out[part, b, c, b, 24 * part + c] = 1.0
    return out.reshape(2 * TS * TS, KDIM)


def filter_kernel(template_ref, wedge_ref, right_ref, ahead_ref, back_ref, out_ref):
    def product(a, b):
        return jnp.dot(a, b, precision=EXACT, preferred_element_type=jnp.float32)

    width = TS * TS
    spec = product(template_ref[...], right_ref[...])
    spec = jnp.concatenate([spec[:, :width], spec[:, width:]], axis=0)
    keep = wedge_ref[...]
    spec = product(ahead_ref[...], spec) * jnp.concatenate([keep, keep], axis=0)
    spec = product(back_ref[...], spec)
    filt = product(spec[:TS], right_ref[:, :width]) + product(spec[TS:], right_ref[:, width:])
    filt = filt * (1.0 / float(TS**3))
    centered = filt - jnp.sum(filt) * (1.0 / float(TS**3))
    normed = centered / jnp.sqrt(jnp.sum(centered * centered) + 1e-05)
    out_ref[...] = jnp.concatenate([normed[:, :LANES], normed[:, LANES:]], axis=0)


def volume_kernel(place_ref, inside_ref, own_ref, across_ref, high_ref, low_ref, scale_ref, spec_ref):
    even = place_ref[1] % 2 == 0
    inside_at = pl.multiple_of(jnp.where(even, 16, 0), 8)
    across_at = pl.multiple_of(16 - inside_at, 8)
    for ref, start in ((inside_ref, inside_at), (own_ref, 8), (across_ref, across_at)):
        for lane in range(0, NY, LANES):
            bins = forward([ref[x, :, lane : lane + LANES] for x in range(NF)])
            for k, (re, im) in enumerate(slots(bins)):
                spec_ref[k, pl.ds(start, 8), lane : lane + LANES] = re
                spec_ref[k, pl.ds(start + 24, 8), lane : lane + LANES] = im

    def split(k, carry):
        high_ref[k], low_ref[k] = halves(spec_ref[k])
        return carry

    lax.fori_loop(0, NK, split, 0)
    first = place_ref[0] * STRIP
    sums = []
    for x in range(STRIP + TS - 1):
        inside, across = inside_ref[first + x], across_ref[first + x]
        layers = jnp.concatenate(
            [jnp.where(even, across, inside), own_ref[first + x], jnp.where(even, inside, across)], axis=0
        )
        sums.append(layers * layers)
    for step in (1, 2, 4, 8):
        sums = [sums[i] + sums[i + step] for i in range(len(sums) - step)]
    for x in range(STRIP):
        total = sums[x]
        for step in (1, 2, 4, 8):
            total = total + pltpu.roll(total, 24 - step, axis=0)
        total = total[:SLAB]
        for step in (1, 2, 4, 8):
            total = total + pltpu.roll(total, NY - step, axis=1)
        total = pltpu.roll(total, HALF, axis=1)
        scale_ref[x] = (1.0 / NF) / jnp.sqrt(total * (1.0 / float(TS**3)) + 1e-05)


def score_kernel(
    place_ref, a_ref, b_ref, spread_ref, high_ref, low_ref,
    out0_ref, out1_ref, out2_ref, out3_ref,
    spec_ref, base_ref, left_a, left_b, high_a, high_b, low_a, low_b, prod_ref, best_ref,
):
    width = TS * TS
    for lane in range(0, width, LANES):
        start = lane // LANES * TS
        groups = []
        for ref in (a_ref, b_ref):
            rows = [ref[pl.ds(start + a, 8, stride=2 * TS), :] for a in range(TS)]
            groups.append(slots(forward(rows + [None] * (NF - TS))))
        for k, ((re0, im0), (re1, im1)) in enumerate(zip(*groups)):
            re = halves(jnp.concatenate([re0, re1], axis=0))
            im = halves(jnp.concatenate([im0, im1], axis=0))
            for h in range(2):
                row, nil = 64 * k + 32 * h, jnp.zeros_like(re[h])
                left, right = slice(lane, lane + LANES), slice(width + lane, width + lane + LANES)
                spec_ref[row : row + NO, left] = re[h]
                spec_ref[row : row + NO, right] = nil if k == 0 else im[h]
                spec_ref[row + NO : row + 2 * NO, left] = nil if k == 0 else -im[h]
                spec_ref[row + NO : row + 2 * NO, right] = im[h] if k == 0 else re[h]

    def expand(i, carry):
        row = pl.multiple_of(i * 256, 256)
        base_ref[pl.ds(row, 256), :] = jnp.dot(
            spec_ref[pl.ds(row, 256), :], spread_ref[...], preferred_element_type=jnp.float32
        ).astype(jnp.bfloat16)
        return carry

    lax.fori_loop(0, 4, expand, 0)

    def build(k, left, right_high, right_low):
        for h in range(2):
            for part in range(2):
                at = pl.multiple_of(k * 64 + 32 * h + 16 * part, 16)
                value = base_ref[pl.ds(at, NO), :]
                for z in range(SLAB):
                    row = h * 256 + part * 128 + z * NO
                    left[row : row + NO, :] = value if z == 0 else pltpu.roll(value, z, axis=1)
        for src, dst in ((high_ref, right_high), (low_ref, right_low)):
            value = src[k]
            for b in range(TS):
                shift = (HALF - b) % NY
                dst[48 * b : 48 * b + 48, :] = value if shift == 0 else pltpu.roll(value, shift, axis=1)

    def multiply(k, left, right_high, right_low):
        both = jnp.dot(left[...], right_high[...], preferred_element_type=jnp.float32)
        low = jnp.dot(left[:256], right_low[...], preferred_element_type=jnp.float32)
        prod_ref[k] = both[:256] + (both[256:] + low)

    first, second = (left_a, high_a, low_a), (left_b, high_b, low_b)
    build(0, *first)

    def two(i, carry):
        k = 2 * i
        multiply(k, *first)
        build(k + 1, *second)
        multiply(k + 1, *second)
        build(jnp.minimum(k + 2, NK - 1), *first)
        return carry

    lax.fori_loop(0, NK // 2, two, 0)
    best_ref[...] = jnp.zeros_like(best_ref)

    def finish(z, carry):
        row = pl.multiple_of(z * NO, NO)
        here = lax.broadcasted_iota(jnp.int32, (SLAB, LANES), 0) == z
        for lane in range(0, NY, LANES):
            top = None
            for o in (0, 8):
                pairs = [
                    (
                        prod_ref[k, pl.ds(row + o, 8), lane : lane + LANES],
                        prod_ref[k, pl.ds(128 + row + o, 8), lane : lane + LANES],
                    )
                    for k in range(NK)
                ]
                rows = inverse(unslot(pairs), NF, NF // 2)
                top = rows if top is None else [jnp.maximum(a, b) for a, b in zip(top, rows)]
            for x in range(NF // 2):
                largest = jnp.max(top[x], axis=0, keepdims=True)
                best_ref[x, :, lane : lane + LANES] = jnp.where(
                    here, largest, best_ref[x, :, lane : lane + LANES]
                )
        return carry

    lax.fori_loop(0, SLAB, finish, 0)
    mine = place_ref[0]
    for m, ref in enumerate((out0_ref, out1_ref, out2_ref, out3_ref)):
        ref[...] = best_ref[pl.ds((mine ^ m) * STRIP, STRIP)]


def last_kernel(scale_ref, a_ref, b_ref, c_ref, d_ref, out_ref):
    for x in range(STRIP):
        top = jnp.maximum(jnp.maximum(a_ref[x], b_ref[x]), jnp.maximum(c_ref[x], d_ref[x]))
        out_ref[:, x, :] = top * scale_ref[x]


def call(kernel, outs, scratch, args, specs, flops=0, nbytes=0):
    return pl.pallas_call(
        kernel,
        out_shape=outs,
        in_specs=specs,
        out_specs=[VMEM] * len(outs) if isinstance(outs, (list, tuple)) else VMEM,
        scratch_shapes=scratch,
        compiler_params=pltpu.CompilerParams(vmem_limit_bytes=48 * 1024 * 1024),
        cost_estimate=pl.CostEstimate(flops=flops, bytes_accessed=nbytes, transcendentals=0),
    )(*args)


def shards(volume, templates, wedge):
    f32, bf16 = jnp.float32, jnp.bfloat16
    count = lax.axis_size("orient")
    me = lax.axis_index("orient")
    place = jnp.stack([me % GROUP, lax.axis_index("zslab")]).astype(jnp.int32)
    region = me // GROUP

    def swap(value, mask):
        return lax.ppermute(value, "orient", [(i, i ^ mask) for i in range(count)])

    template = jnp.transpose(templates[0], (1, 2, 0)).reshape(TS, TS * TS)
    keep = jnp.transpose(wedge.astype(f32), (1, 2, 0)).reshape(TS, TS * TS)
    normed = call(
        filter_kernel, jax.ShapeDtypeStruct((2 * TS, LANES), f32), [],
        (template, keep) + filter_tables(), [VMEM] * 5, 1 << 22, 1 << 20,
    )
    near = [[8 * a + b for a in range(8)] for b in range(8)]
    eight = lax.all_to_all(
        jnp.broadcast_to(normed, (8, 2 * TS, LANES)), "orient", 0, 0, tiled=True, axis_index_groups=near
    ).reshape(16 * TS, LANES)
    gathered = [eight, swap(eight, 4)]

    rows = volume.shape[1]
    pieces = [
        lax.dynamic_slice_in_dim(volume, (region * 16 - HALF + 8 * j) % rows, 8, 1) for j in range(4)
    ]
    window = jnp.transpose(jnp.concatenate(pieces, axis=1), (1, 0, 2))
    slabs = lax.axis_size("zslab")
    inside = lax.ppermute(window, "zslab", [(s, s ^ 1) for s in range(slabs)])
    across = lax.ppermute(window, "zslab", [(1, 2), (2, 1)])
    high, low, scale = call(
        volume_kernel,
        (
            jax.ShapeDtypeStruct((NK, 48, NY), bf16),
            jax.ShapeDtypeStruct((NK, 48, NY), bf16),
            jax.ShapeDtypeStruct((STRIP, SLAB, NY), f32),
        ),
        [pltpu.VMEM((NK, 48, NY), f32)],
        (place, inside, window, across), [SMEM] + [VMEM] * 3, 1 << 24, 1 << 21,
    )
    spread = jnp.asarray(spread_table(), bf16)
    strip = jax.ShapeDtypeStruct((STRIP, SLAB, NY), f32)
    parts = call(
        score_kernel, (strip,) * 4,
        [
            pltpu.VMEM((NK * 64, 2 * TS * TS), bf16),
            pltpu.VMEM((NK * 64, KDIM), bf16),
            pltpu.VMEM((512, KDIM), bf16),
            pltpu.VMEM((512, KDIM), bf16),
            pltpu.VMEM((KDIM, NY), bf16),
            pltpu.VMEM((KDIM, NY), bf16),
            pltpu.VMEM((KDIM, NY), bf16),
            pltpu.VMEM((KDIM, NY), bf16),
            pltpu.VMEM((NK, 256, NY), f32),
            pltpu.VMEM((NF // 2, SLAB, NY), f32),
        ],
        (place, *gathered, spread, high, low), [SMEM] + [VMEM] * 5, 1 << 33, 1 << 21,
    )
    arrived = [parts[0]] + [swap(parts[m], m) for m in range(1, GROUP)]
    return call(
        last_kernel, jax.ShapeDtypeStruct((SLAB, STRIP, NY), f32), [],
        (scale, *arrived), [VMEM] * 5, 1 << 16, 1 << 18,
    )


def solution(mesh):
    return jax.shard_map(
        shards,
        mesh=mesh,
        in_specs=(P("zslab", None, None), P("orient", None, None, None), P()),
        out_specs=P("zslab", "orient", None),
        check_vma=False,
    )
```

```python
import math

import jax
import jax.numpy as jnp
import numpy as np
from jax import lax
from jax.experimental import pallas as pl
from jax.experimental.pallas import tpu as pltpu
from jax.sharding import PartitionSpec as P

TS = 16
HALF = 8
NF = 32
NK = 16
SLAB = 8
NY = 256
GROUP = 4
NO = 16
STRIP = 4
LANES = 128
KDIM = TS * 48
EXACT = lax.Precision.HIGHEST
VMEM = pl.BlockSpec(memory_space=pltpu.VMEM)
HBM = pl.BlockSpec(memory_space=pltpu.HBM)


def plus(a, b):
    if a is None:
        return b
    return a if b is None else a + b


def minus(a, b):
    if b is None:
        return a
    return -b if a is None else a - b


def twiddled(value, k, count, sign):
    re, im = value
    if k == 0:
        return value
    if 4 * k == count:
        return (None if im is None else -sign * im, None if re is None else sign * re)
    c = math.cos(2.0 * math.pi * k / count)
    s = sign * math.sin(2.0 * math.pi * k / count)
    if im is None:
        return (c * re, s * re)
    if re is None:
        return (-s * im, c * im)
    return (c * re - s * im, s * re + c * im)


def forward(rows):
    count = len(rows)
    if count == 2:
        return [(plus(rows[0], rows[1]), None), (minus(rows[0], rows[1]), None)]
    even, odd = forward(rows[::2]), forward(rows[1::2])
    bins = [None] * (count // 2 + 1)
    for k in range(count // 4 + 1):
        e, o = even[k], twiddled(odd[k], k, count, -1.0)
        bins[k] = (plus(e[0], o[0]), plus(e[1], o[1]))
        if 4 * k != count:
            re, im = minus(e[0], o[0]), minus(e[1], o[1])
            bins[count // 2 - k] = (re, None if im is None else -im)
    return bins


def inverse(bins, count, need):
    if count == 2:
        first = bins[0][0] + bins[1][0]
        return [first] if need == 1 else [first, bins[0][0] - bins[1][0]]
    even, odd = [], []
    for k in range(count // 4 + 1):
        a, b = bins[k], bins[count // 2 - k]
        if k == 0:
            even.append((a[0] + b[0], None))
            odd.append((a[0] - b[0], None))
        elif 4 * k == count:
            even.append((2.0 * a[0], None))
            odd.append((-2.0 * a[1], None))
        else:
            even.append((a[0] + b[0], a[1] - b[1]))
            odd.append(twiddled((a[0] - b[0], a[1] + b[1]), k, count, 1.0))
    evens = inverse(even, count // 2, (need + 1) // 2)
    odds = inverse(odd, count // 2, need // 2)
    rows = [None] * need
    rows[::2] = evens
    rows[1::2] = odds
    return rows


def slots(bins):
    return [(bins[0][0], bins[NK][0])] + [bins[k] for k in range(1, NK)]


def unslot(pairs):
    return [(pairs[0][0], None)] + list(pairs[1:]) + [(pairs[0][1], None)]


def halves(value):
    high = value.astype(jnp.bfloat16)
    return high, (value - high.astype(jnp.float32)).astype(jnp.bfloat16)


def two_terms(table):
    high = np.asarray(table, jnp.bfloat16)
    return np.stack([high, np.asarray(table - high.astype(np.float64), jnp.bfloat16)])


def filter_tables():
    small = np.arange(TS)
    pair = 2.0 * math.pi * np.outer(small, small) / TS
    two = pair[:, None, :, None] + pair[None, :, None, :]
    two = two.reshape(TS * TS, TS * TS)
    right = np.concatenate([np.cos(two), -np.sin(two)], axis=1)
    c, s = np.cos(pair), np.sin(pair)
    ahead = np.block([[c, s], [-s, c]])
    back = np.block([[c, -s], [s, c]])
    return two_terms(right), np.float32(np.stack([ahead, back]))


def spread_table():
    out = np.zeros((TS, TS, TS, 24), np.float32)
    for b in range(TS):
        for c in range(TS):
            out[c, b, b, c] = 1.0
    return out.reshape(TS * TS, KDIM // 2)


def front_kernel(
    template_hbm, wedge_hbm, right_hbm, small_hbm, out_ref,
    template_ref, wedge_ref, right_ref, small_ref, sems,
):
    width = TS * TS
    copies = [
        pltpu.make_async_copy(src, dst, sems.at[i])
        for i, (src, dst) in enumerate(
            ((template_hbm, template_ref), (right_hbm, right_ref), (small_hbm, small_ref), (wedge_hbm, wedge_ref))
        )
    ]
    for copy in copies:
        copy.start()

    def flat(ref):
        return jnp.concatenate([ref[c].astype(jnp.float32) for c in range(TS)], axis=1)

    def exact(a, b):
        return jnp.dot(a, b, precision=EXACT, preferred_element_type=jnp.float32)

    def product(value, lanes):
        rows = value.shape[0]
        both = jnp.concatenate(halves(value), axis=0)
        out = jnp.dot(both, right_ref[0, :, lanes], preferred_element_type=jnp.float32)
        low = jnp.dot(both[:rows], right_ref[1, :, lanes], preferred_element_type=jnp.float32)
        return out[:rows] + (out[rows:] + low)

    for copy in copies:
        copy.wait()
    spec = product(flat(template_ref), slice(0, 2 * width))
    spec = jnp.concatenate([spec[:, :width], spec[:, width:]], axis=0)
    keep = flat(wedge_ref)
    spec = exact(small_ref[0], spec) * jnp.concatenate([keep, keep], axis=0)
    spec = exact(small_ref[1], spec)
    filt = product(spec[:TS], slice(0, width)) + product(spec[TS:], slice(width, 2 * width))
    filt = filt * (1.0 / float(TS**3))
    centered = filt - jnp.sum(filt) * (1.0 / float(TS**3))
    out_ref[...] = centered / jnp.sqrt(jnp.sum(centered * centered) + 1e-05)


def window_kernel(after_ref, volume_hbm, window_ref, piece_ref, sems):
    rows = volume_hbm.shape[1]
    first = lax.axis_index("orient") // GROUP * 16 + (rows - HALF)
    pieces = []
    for j in range(NF // 8):
        at = pl.multiple_of(lax.rem(first + 8 * j, rows), 8)
        for h in range(NY // LANES):
            copy = pltpu.make_async_copy(
                volume_hbm.at[:, pl.ds(at, 8), pl.ds(h * LANES, LANES)],
                piece_ref.at[h, :, pl.ds(8 * j, 8), :],
                sems.at[len(pieces)],
            )
            copy.start()
            pieces.append(copy)
    for copy in pieces:
        copy.wait()
    flat_piece = piece_ref.reshape(NY // LANES, SLAB * NF, LANES)
    for h in range(NY // LANES):
        for x in range(NF):
            window_ref[x, :, h * LANES : (h + 1) * LANES] = flat_piece[h, pl.ds(x, SLAB, stride=NF), :]


def volume_kernel(inside_ref, own_ref, across_ref, high_ref, low_ref, spec_ref):
    even = lax.rem(lax.axis_index("zslab"), 2) == 0
    inside_at = pl.multiple_of(jnp.where(even, 16, 0), 8)
    across_at = pl.multiple_of(16 - inside_at, 8)
    for ref, start in ((inside_ref, inside_at), (own_ref, 8), (across_ref, across_at)):
        for lane in range(0, NY, LANES):
            bins = forward([ref[x, :, lane : lane + LANES] for x in range(NF)])
            for k, (re, im) in enumerate(slots(bins)):
                spec_ref[k, pl.ds(start, 8), lane : lane + LANES] = re
                spec_ref[k, pl.ds(start + 24, 8), lane : lane + LANES] = im

    def split(k, carry):
        nil = jnp.zeros((8, NY), jnp.float32)
        for part in range(2):
            a, b, c = (spec_ref[k, 24 * part + 8 * j : 24 * part + 8 * j + 8, :] for j in range(3))
            rows = slice(64 * part, 64 * part + 64)
            high_ref[k, rows], low_ref[k, rows] = halves(
                jnp.concatenate([a, b, c, nil, nil, a, b, c], axis=0)
            )
        return carry

    lax.fori_loop(0, NK, split, 0)


def scale_kernel(inside_ref, own_ref, across_ref, scale_ref):
    even = lax.rem(lax.axis_index("zslab"), 2) == 0
    first = lax.rem(lax.axis_index("orient"), GROUP) * STRIP
    sums = []
    for x in range(STRIP + TS - 1):
        inside, across = inside_ref[first + x], across_ref[first + x]
        layers = jnp.concatenate(
            [jnp.where(even, across, inside), own_ref[first + x], jnp.where(even, inside, across)], axis=0
        )
        sums.append(layers * layers)
    for step in (1, 2, 4, 8):
        sums = [sums[i] + sums[i + step] for i in range(len(sums) - step)]
    for x in range(STRIP):
        total = sums[x]
        for step in (1, 2, 4, 8):
            total = total + pltpu.roll(total, 24 - step, axis=0)
        total = total[:SLAB]
        for step in (1, 2, 4, 8):
            total = total + pltpu.roll(total, NY - step, axis=1)
        total = pltpu.roll(total, HALF, axis=1)
        scale_ref[x] = (1.0 / NF) / jnp.sqrt(total * (1.0 / float(TS**3)) + 1e-05)


def score_kernel(
    gathered_ref, spread_ref, high_ref, low_ref,
    out0_ref, out1_ref, out2_ref, out3_ref,
    wide_ref, base_ref, left_a, left_b, high_a, high_b, low_a, low_b, prod_ref, best_ref,
):
    side = KDIM // 2
    high, low = halves(gathered_ref[...])
    wide = jnp.dot(high, spread_ref[...], preferred_element_type=jnp.float32) + jnp.dot(
        low, spread_ref[...], preferred_element_type=jnp.float32
    )
    for j in range(side // LANES):
        wide_ref[j] = wide[:, j * LANES : (j + 1) * LANES]
    for j in range(side // LANES):
        groups = []
        for o in (0, 8):
            rows = [wide_ref[j, pl.ds(o * TS + a, 8, stride=TS), :] for a in range(TS)]
            groups.append(slots(forward(rows + [None] * (NF - TS))))
        for k, ((re0, im0), (re1, im1)) in enumerate(zip(*groups)):
            re = halves(jnp.concatenate([re0, re1], axis=0))
            im = halves(jnp.concatenate([im0, im1], axis=0))
            for h in range(2):
                base_ref[k, h, 0, :, j * LANES : (j + 1) * LANES] = re[h]
                base_ref[k, h, 1, :, j * LANES : (j + 1) * LANES] = im[h]

    def turned(value, shift, axis=1):
        shift = shift % value.shape[axis]
        return value if shift == 0 else pltpu.roll(value, shift, axis=axis)

    def build(k, left, right_high, right_low):
        for h in range(2):
            re, im = base_ref[k, h, 0], base_ref[k, h, 1]
            for z in range(SLAB):
                row = h * 256 + z * NO
                rows, more = slice(row, row + NO), slice(row + 128, row + 128 + NO)
                re_z, im_z = turned(re, z), turned(im, z)
                left[rows, :side] = re_z
                if isinstance(k, int) and k == 0:
                    nil = jnp.zeros_like(re_z)
                    left[rows, side:] = nil
                    left[more, :side] = nil
                    left[more, side:] = im_z
                else:
                    left[rows, side:] = im_z
                    left[more, :side] = -im_z
                    left[more, side:] = re_z
        for src, dst in ((high_ref, right_high), (low_ref, right_low)):
            for part in range(2):
                a, b, c, d = (src[k, 64 * part + 16 * j : 64 * part + 16 * j + 16, :] for j in range(4))
                for y in range(0, TS, 2):
                    row = side * part + 24 * y
                    here, after = HALF - y, HALF - y - 1
                    dst[row : row + 16, :] = turned(a, here)
                    dst[row + 16 : row + 32, :] = turned(b, here) + turned(c, after)
                    dst[row + 32 : row + 48, :] = turned(d, after)

    def multiply(k, left, right_high, right_low):
        both = jnp.dot(left[...], right_high[...], preferred_element_type=jnp.float32)
        low = jnp.dot(left[:256], right_low[...], preferred_element_type=jnp.float32)
        prod_ref[k] = both[:256] + (both[256:] + low)

    first, second = (left_a, high_a, low_a), (left_b, high_b, low_b)
    build(0, *first)

    def two(i, carry):
        k = 2 * i
        multiply(k, *first)
        build(k + 1, *second)
        multiply(k + 1, *second)
        build(jnp.minimum(k + 2, NK - 1), *first)
        return carry

    lax.fori_loop(0, NK // 2, two, 0)
    best_ref[...] = jnp.zeros_like(best_ref)

    def finish(z, carry):
        row = pl.multiple_of(z * NO, NO)
        here = lax.broadcasted_iota(jnp.int32, (SLAB, LANES), 0) == z
        for lane in range(0, NY, LANES):
            top = None
            for o in (0, 8):
                pairs = [
                    (
                        prod_ref[k, pl.ds(row + o, 8), lane : lane + LANES],
                        prod_ref[k, pl.ds(128 + row + o, 8), lane : lane + LANES],
                    )
                    for k in range(NK)
                ]
                rows = inverse(unslot(pairs), NF, NF // 2)
                top = rows if top is None else [jnp.maximum(a, b) for a, b in zip(top, rows)]
            for x in range(NF // 2):
                largest = jnp.max(top[x], axis=0, keepdims=True)
                best_ref[x, :, lane : lane + LANES] = jnp.where(
                    here, largest, best_ref[x, :, lane : lane + LANES]
                )
        return carry

    lax.fori_loop(0, SLAB, finish, 0)
    mine = lax.rem(lax.axis_index("orient"), GROUP)
    for m, ref in enumerate((out0_ref, out1_ref, out2_ref, out3_ref)):
        ref[...] = best_ref[pl.ds((mine ^ m) * STRIP, STRIP)]


def last_kernel(scale_ref, a_ref, b_ref, c_ref, d_ref, out_ref):
    for x in range(STRIP):
        top = jnp.maximum(jnp.maximum(a_ref[x], b_ref[x]), jnp.maximum(c_ref[x], d_ref[x]))
        out_ref[:, x, :] = top * scale_ref[x]


def call(kernel, outs, scratch, args, specs, flops=0, nbytes=0, limit=48 * 1024 * 1024):
    return pl.pallas_call(
        kernel,
        out_shape=outs,
        in_specs=specs,
        out_specs=[VMEM] * len(outs) if isinstance(outs, (list, tuple)) else VMEM,
        scratch_shapes=scratch,
        compiler_params=pltpu.CompilerParams(vmem_limit_bytes=limit),
        cost_estimate=pl.CostEstimate(flops=flops, bytes_accessed=nbytes, transcendentals=0),
    )(*args)


def shards(volume, templates, wedge):
    f32, bf16 = jnp.float32, jnp.bfloat16
    count = lax.axis_size("orient")
    def swap(value, mask):
        return lax.ppermute(value, "orient", [(i, i ^ mask) for i in range(count)])

    right, small = (jnp.asarray(t) for t in filter_tables())
    normed = call(
        front_kernel, pltpu.VMEM((TS, TS * TS), f32),
        [
            pltpu.VMEM((TS, TS, TS), f32),
            pltpu.VMEM((TS, TS, TS), jnp.int32),
            pltpu.VMEM(right.shape, bf16),
            pltpu.VMEM(small.shape, f32),
            pltpu.SemaphoreType.DMA((4,)),
        ],
        (templates[0], wedge, right, small), [HBM] * 4, 1 << 22, 1 << 20, None,
    )
    other = swap(normed, 4)
    window = call(
        window_kernel, pltpu.VMEM((NF, SLAB, NY), f32),
        [pltpu.VMEM((NY // LANES, SLAB, NF, LANES), f32), pltpu.SemaphoreType.DMA((8,))],
        (normed, volume), [VMEM, HBM], 0, 1 << 19, None,
    )
    fan = jnp.broadcast_to(jnp.concatenate([normed, other], axis=0), (8, 2 * TS, TS * TS))
    near = [[8 * a + b for a in range(8)] for b in range(8)]
    gathered = lax.all_to_all(
        fan, "orient", 0, 0, tiled=True, axis_index_groups=near
    ).reshape(NO * TS, TS * TS)

    slabs = lax.axis_size("zslab")
    inside = lax.ppermute(window, "zslab", [(s, s ^ 1) for s in range(slabs)])
    across = lax.ppermute(window, "zslab", [(1, 2), (2, 1)])
    inside, gathered = lax.optimization_barrier((inside, gathered))
    spectrum = jax.ShapeDtypeStruct((NK, 128, NY), bf16)
    high, low = call(
        volume_kernel, (spectrum, spectrum), [pltpu.VMEM((NK, 48, NY), f32)],
        (inside, window, across), [VMEM] * 3, 1 << 24, 1 << 21,
    )
    spread = jnp.asarray(spread_table(), bf16)
    strip = jax.ShapeDtypeStruct((STRIP, SLAB, NY), f32)
    parts = call(
        score_kernel, (strip,) * 4,
        [
            pltpu.VMEM((KDIM // 2 // LANES, NO * TS, LANES), f32),
            pltpu.VMEM((NK, 2, 2, NO, KDIM // 2), bf16),
            pltpu.VMEM((512, KDIM), bf16),
            pltpu.VMEM((512, KDIM), bf16),
            pltpu.VMEM((KDIM, NY), bf16),
            pltpu.VMEM((KDIM, NY), bf16),
            pltpu.VMEM((KDIM, NY), bf16),
            pltpu.VMEM((KDIM, NY), bf16),
            pltpu.VMEM((NK, 256, NY), f32),
            pltpu.VMEM((NF // 2, SLAB, NY), f32),
        ],
        (gathered, spread, high, low), [VMEM] * 4, 1 << 33, 1 << 21,
    )
    late, _ = lax.optimization_barrier((inside, parts[1]))
    scale = call(
        scale_kernel, strip, [], (late, window, across), [VMEM] * 3, 1 << 22, 1 << 20
    )
    arrived = [parts[0]] + [swap(parts[m], m) for m in range(1, GROUP)]
    return call(
        last_kernel, jax.ShapeDtypeStruct((SLAB, STRIP, NY), f32), [],
        (scale, *arrived), [VMEM] * 5, 1 << 16, 1 << 18,
    )


def solution(mesh):
    return jax.shard_map(
        shards,
        mesh=mesh,
        in_specs=(P("zslab", None, None), P("orient", None, None, None), P()),
        out_specs=P("zslab", "orient", None),
        check_vma=False,
    )
```

```python
import math

import jax
import jax.numpy as jnp
import numpy as np
from jax import lax
from jax.experimental import pallas as pl
from jax.experimental.pallas import tpu as pltpu
from jax.sharding import PartitionSpec as P

TS = 16
HALF = 8
NF = 32
NK = 16
SLAB = 8
NY = 256
GROUP = 4
NO = 16
STRIP = 4
LANES = 128
KDIM = TS * 48
EXACT = lax.Precision.HIGHEST
VMEM = pl.BlockSpec(memory_space=pltpu.VMEM)
HBM = pl.BlockSpec(memory_space=pltpu.HBM)


def plus(a, b):
    if a is None:
        return b
    return a if b is None else a + b


def minus(a, b):
    if b is None:
        return a
    return -b if a is None else a - b


def twiddled(value, k, count, sign):
    re, im = value
    if k == 0:
        return value
    if 4 * k == count:
        return (None if im is None else -sign * im, None if re is None else sign * re)
    c = math.cos(2.0 * math.pi * k / count)
    s = sign * math.sin(2.0 * math.pi * k / count)
    if im is None:
        return (c * re, s * re)
    if re is None:
        return (-s * im, c * im)
    return (c * re - s * im, s * re + c * im)


def forward(rows):
    count = len(rows)
    if count == 2:
        return [(plus(rows[0], rows[1]), None), (minus(rows[0], rows[1]), None)]
    even, odd = forward(rows[::2]), forward(rows[1::2])
    bins = [None] * (count // 2 + 1)
    for k in range(count // 4 + 1):
        e, o = even[k], twiddled(odd[k], k, count, -1.0)
        bins[k] = (plus(e[0], o[0]), plus(e[1], o[1]))
        if 4 * k != count:
            re, im = minus(e[0], o[0]), minus(e[1], o[1])
            bins[count // 2 - k] = (re, None if im is None else -im)
    return bins


def inverse_step(bins, count):
    even, odd = {}, {}
    for k in range(count // 4 + 1):
        if k not in bins:
            continue
        a, b = bins[k], bins[count // 2 - k]
        if k == 0:
            even[k] = (a[0] + b[0], None)
            odd[k] = (a[0] - b[0], None)
        elif 4 * k == count:
            even[k] = (2.0 * a[0], None)
            odd[k] = (-2.0 * a[1], None)
        else:
            even[k] = (a[0] + b[0], a[1] - b[1])
            odd[k] = twiddled((a[0] - b[0], a[1] + b[1]), k, count, 1.0)
    return even, odd


def inverse(bins, count, need):
    if count == 2:
        first = bins[0][0] + bins[1][0]
        return [first] if need == 1 else [first, bins[0][0] - bins[1][0]]
    even, odd = inverse_step(bins, count)
    rows = [None] * need
    rows[::2] = inverse(even, count // 2, (need + 1) // 2)
    rows[1::2] = inverse(odd, count // 2, need // 2)
    return rows


def slots(bins):
    return [(bins[0][0], bins[NK][0])] + [bins[k] for k in range(1, NK)]


QUADS = ((0, 4, 8, 12), (1, 7, 9, 15), (2, 6, 10, 14), (3, 5, 11, 13))


def halves(value):
    high = value.astype(jnp.bfloat16)
    return high, (value - high.astype(jnp.float32)).astype(jnp.bfloat16)


def two_terms(table):
    high = np.asarray(table, jnp.bfloat16)
    return np.stack([high, np.asarray(table - high.astype(np.float64), jnp.bfloat16)])


def filter_tables():
    small = np.arange(TS)
    pair = 2.0 * math.pi * np.outer(small, small) / TS
    two = pair[:, None, :, None] + pair[None, :, None, :]
    two = two.reshape(TS * TS, TS * TS)
    right = np.concatenate([np.cos(two), -np.sin(two)], axis=1)
    c, s = np.cos(pair), np.sin(pair)
    ahead = np.block([[c, s], [-s, c]])
    back = np.block([[c, -s], [s, c]])
    return two_terms(right), np.float32(np.stack([ahead, back]))


def spread_table():
    out = np.zeros((TS, TS, TS, 24), np.float32)
    for b in range(TS):
        for c in range(TS):
            out[c, b, b, c] = 1.0
    return out.reshape(TS * TS, KDIM // 2)


def front_kernel(
    template_hbm, wedge_hbm, right_hbm, small_hbm, out_ref, token_ref,
    template_ref, wedge_ref, right_ref, small_ref, sems,
):
    width = TS * TS
    copies = [
        pltpu.make_async_copy(src, dst, sems.at[i])
        for i, (src, dst) in enumerate(
            ((template_hbm, template_ref), (right_hbm, right_ref), (small_hbm, small_ref), (wedge_hbm, wedge_ref))
        )
    ]
    for copy in copies:
        copy.start()

    def flat(ref):
        return jnp.concatenate([ref[c].astype(jnp.float32) for c in range(TS)], axis=1)

    def exact(a, b):
        return jnp.dot(a, b, precision=EXACT, preferred_element_type=jnp.float32)

    def product(value, lanes):
        rows = value.shape[0]
        both = jnp.concatenate(halves(value), axis=0)
        out = jnp.dot(both, right_ref[0, :, lanes], preferred_element_type=jnp.float32)
        low = jnp.dot(both[:rows], right_ref[1, :, lanes], preferred_element_type=jnp.float32)
        return out[:rows] + (out[rows:] + low)

    for copy in copies:
        copy.wait()
    spec = product(flat(template_ref), slice(0, 2 * width))
    spec = jnp.concatenate([spec[:, :width], spec[:, width:]], axis=0)
    keep = flat(wedge_ref)
    spec = exact(small_ref[0], spec) * jnp.concatenate([keep, keep], axis=0)
    spec = exact(small_ref[1], spec)
    filt = product(spec[:TS], slice(0, width)) + product(spec[TS:], slice(width, 2 * width))
    filt = filt * (1.0 / float(TS**3))
    centered = filt - jnp.sum(filt) * (1.0 / float(TS**3))
    out_ref[...] = centered / jnp.sqrt(jnp.sum(centered * centered) + 1e-05)
    token_ref[...] = jnp.zeros_like(token_ref)


def window_kernel(after_ref, volume_hbm, window_ref, piece_ref, sems):
    rows = volume_hbm.shape[1]
    first = lax.axis_index("orient") // GROUP * 16 + (rows - HALF)
    pieces = []
    for j in range(NF // 8):
        at = pl.multiple_of(lax.rem(first + 8 * j, rows), 8)
        for h in range(NY // LANES):
            copy = pltpu.make_async_copy(
                volume_hbm.at[:, pl.ds(at, 8), pl.ds(h * LANES, LANES)],
                piece_ref.at[h, :, pl.ds(8 * j, 8), :],
                sems.at[len(pieces)],
            )
            copy.start()
            pieces.append(copy)
    for copy in pieces:
        copy.wait()
    flat_piece = piece_ref.reshape(NY // LANES, SLAB * NF, LANES)
    for h in range(NY // LANES):
        for x in range(NF):
            window_ref[x, :, h * LANES : (h + 1) * LANES] = flat_piece[h, pl.ds(x, SLAB, stride=NF), :]


def fan_kernel(own_ref, other_ref, out_ref):
    own, other = own_ref[...], other_ref[...]
    for i in range(out_ref.shape[0]):
        out_ref[i, :TS], out_ref[i, TS:] = own, other


def volume_kernel(inside_ref, own_ref, across_ref, high_ref, low_ref, spec_ref):
    even = lax.rem(lax.axis_index("zslab"), 2) == 0
    inside_at = pl.multiple_of(jnp.where(even, 16, 0), 8)
    across_at = pl.multiple_of(16 - inside_at, 8)
    for ref, start in ((inside_ref, inside_at), (own_ref, 8), (across_ref, across_at)):
        for lane in range(0, NY, LANES):
            bins = forward([ref[x, :, lane : lane + LANES] for x in range(NF)])
            for k, (re, im) in enumerate(slots(bins)):
                spec_ref[k, pl.ds(start, 8), lane : lane + LANES] = re
                spec_ref[k, pl.ds(start + 24, 8), lane : lane + LANES] = im

    def split(k, carry):
        nil = jnp.zeros((8, NY), jnp.float32)
        for part in range(2):
            a, b, c = (spec_ref[k, 24 * part + 8 * j : 24 * part + 8 * j + 8, :] for j in range(3))
            rows = slice(64 * part, 64 * part + 64)
            high_ref[k, rows], low_ref[k, rows] = halves(
                jnp.concatenate([a, b, c, nil, nil, a, b, c], axis=0)
            )
        return carry

    lax.fori_loop(0, NK, split, 0)


def scale_kernel(inside_ref, own_ref, across_ref, scale_ref):
    even = lax.rem(lax.axis_index("zslab"), 2) == 0
    first = lax.rem(lax.axis_index("orient"), GROUP) * STRIP
    sums = []
    for x in range(STRIP + TS - 1):
        inside, across = inside_ref[first + x], across_ref[first + x]
        layers = jnp.concatenate(
            [jnp.where(even, across, inside), own_ref[first + x], jnp.where(even, inside, across)], axis=0
        )
        sums.append(layers * layers)
    for step in (1, 2, 4, 8):
        sums = [sums[i] + sums[i + step] for i in range(len(sums) - step)]
    for x in range(STRIP):
        total = sums[x]
        for step in (1, 2, 4, 8):
            total = total + pltpu.roll(total, 24 - step, axis=0)
        total = total[:SLAB]
        for step in (1, 2, 4, 8):
            total = total + pltpu.roll(total, NY - step, axis=1)
        total = pltpu.roll(total, HALF, axis=1)
        scale_ref[x] = (1.0 / NF) / jnp.sqrt(total * (1.0 / float(TS**3)) + 1e-05)


def score_kernel(
    gathered_ref, spread_ref, high_ref, low_ref,
    out0_ref, out1_ref, out2_ref, out3_ref,
    wide_ref, base_ref, left_a, left_b, high_a, high_b, low_a, low_b, prod_a, prod_b, part_ref, best_ref,
):
    side = KDIM // 2
    high, low = halves(gathered_ref[...])
    wide = jnp.dot(high, spread_ref[...], preferred_element_type=jnp.float32) + jnp.dot(
        low, spread_ref[...], preferred_element_type=jnp.float32
    )
    for j in range(side // LANES):
        wide_ref[j] = wide[:, j * LANES : (j + 1) * LANES]
    for j in range(side // LANES):
        groups = []
        for o in (0, 8):
            rows = [wide_ref[j, pl.ds(o * TS + a, 8, stride=TS), :] for a in range(TS)]
            groups.append(slots(forward(rows + [None] * (NF - TS))))
        for k, ((re0, im0), (re1, im1)) in enumerate(zip(*groups)):
            re = halves(jnp.concatenate([re0, re1], axis=0))
            im = halves(jnp.concatenate([im0, im1], axis=0))
            for h in range(2):
                base_ref[k, h, 0, :, j * LANES : (j + 1) * LANES] = re[h]
                base_ref[k, h, 1, :, j * LANES : (j + 1) * LANES] = im[h]

    def turned(value, shift, axis=1):
        shift = shift % value.shape[axis]
        return value if shift == 0 else pltpu.roll(value, shift, axis=axis)

    def build(k, left, right_high, right_low):
        for h in range(2):
            re, im = base_ref[k, h, 0], base_ref[k, h, 1]
            for z in range(SLAB):
                row = h * 256 + z * NO
                rows, more = slice(row, row + NO), slice(row + 128, row + 128 + NO)
                re_z, im_z = turned(re, z), turned(im, z)
                left[rows, :side] = re_z
                if k == 0:
                    nil = jnp.zeros_like(re_z)
                    left[rows, side:] = nil
                    left[more, :side] = nil
                    left[more, side:] = im_z
                else:
                    left[rows, side:] = im_z
                    left[more, :side] = -im_z
                    left[more, side:] = re_z
        for src, dst in ((high_ref, right_high), (low_ref, right_low)):
            for part in range(2):
                a, b, c, d = (src[k, 64 * part + 16 * j : 64 * part + 16 * j + 16, :] for j in range(4))
                for y in range(0, TS, 2):
                    row = side * part + 24 * y
                    here, after = HALF - y, HALF - y - 1
                    dst[row : row + 16, :] = turned(a, here)
                    dst[row + 16 : row + 32, :] = turned(b, here) + turned(c, after)
                    dst[row + 32 : row + 48, :] = turned(d, after)

    def multiply(prod, left, right_high, right_low):
        both = jnp.dot(left[...], right_high[...], preferred_element_type=jnp.float32)
        low = jnp.dot(left[:256], right_low[...], preferred_element_type=jnp.float32)
        prod[...] = both[:256] + (both[256:] + low)

    def combine(quad, prod, groups):
        for group in groups:
            row, lane = group // 2 * 8, group % 2 * LANES
            bins = {}
            for j, k in enumerate(QUADS[quad]):
                re, im = (prod[j, r : r + 8, lane : lane + LANES] for r in (row, 128 + row))
                if k == 0:
                    bins[0], bins[NK] = (re, None), (im, None)
                else:
                    bins[k] = (re, im)
            for i, one in enumerate(inverse_step(bins, NF)):
                for j, two in enumerate(inverse_step(one, NF // 2)):
                    pair = (two[0][0], two[4][0]) if quad == 0 else two[quad]
                    for part in range(2):
                        part_ref[quad, i + 2 * j, part, row : row + 8, lane : lane + LANES] = pair[part]

    order = [k for quad in QUADS for k in quad]
    slot = ((left_a, high_a, low_a), (left_b, high_b, low_b))
    prods = (prod_a, prod_b)
    build(order[0], *slot[0])
    for i in range(NK):
        multiply(prods[i // 4 % 2].at[i % 4], *slot[i % 2])
        if i + 1 < NK:
            build(order[i + 1], *slot[(i + 1) % 2])
        if i >= 4:
            combine(i // 4 - 1, prods[(i // 4 - 1) % 2], range(8 * (i % 4), 8 * (i % 4) + 8))
    combine(3, prods[1], range(32))
    best_ref[...] = jnp.zeros_like(best_ref)

    def finish(z, carry):
        row = pl.multiple_of(z * NO, NO)
        here = lax.broadcasted_iota(jnp.int32, (SLAB, LANES), 0) == z
        for lane in range(0, NY, LANES):
            for sub in range(4):
                top = None
                for o in (0, 8):
                    pairs = [
                        tuple(part_ref[q, sub, p, pl.ds(row + o, 8), lane : lane + LANES] for p in range(2))
                        for q in range(4)
                    ]
                    bins = {0: (pairs[0][0], None), 4: (pairs[0][1], None)}
                    bins.update({q: pairs[q] for q in range(1, 4)})
                    rows = inverse(bins, 8, 4)
                    top = rows if top is None else [jnp.maximum(a, b) for a, b in zip(top, rows)]
                for m in range(4):
                    x = 4 * m + sub
                    largest = jnp.max(top[m], axis=0, keepdims=True)
                    best_ref[x, :, lane : lane + LANES] = jnp.where(
                        here, largest, best_ref[x, :, lane : lane + LANES]
                    )
        return carry

    lax.fori_loop(0, SLAB, finish, 0)
    mine = lax.rem(lax.axis_index("orient"), GROUP)
    for m, ref in enumerate((out0_ref, out1_ref, out2_ref, out3_ref)):
        ref[...] = best_ref[pl.ds((mine ^ m) * STRIP, STRIP)]


def last_kernel(scale_ref, a_ref, b_ref, c_ref, d_ref, out_ref):
    for x in range(STRIP):
        top = jnp.maximum(jnp.maximum(a_ref[x], b_ref[x]), jnp.maximum(c_ref[x], d_ref[x]))
        out_ref[:, x, :] = top * scale_ref[x]


def call(kernel, outs, scratch, args, specs, flops=0, nbytes=0, limit=48 * 1024 * 1024):
    return pl.pallas_call(
        kernel,
        out_shape=outs,
        in_specs=specs,
        out_specs=[VMEM] * len(outs) if isinstance(outs, (list, tuple)) else VMEM,
        scratch_shapes=scratch,
        compiler_params=pltpu.CompilerParams(vmem_limit_bytes=limit),
        cost_estimate=pl.CostEstimate(flops=flops, bytes_accessed=nbytes, transcendentals=0),
    )(*args)


def shards(volume, templates, wedge):
    f32, bf16 = jnp.float32, jnp.bfloat16
    count = lax.axis_size("orient")
    def swap(value, mask):
        return lax.ppermute(value, "orient", [(i, i ^ mask) for i in range(count)])

    right, small = (jnp.asarray(t) for t in filter_tables())
    normed, token = call(
        front_kernel, (pltpu.VMEM((TS, TS * TS), f32), pltpu.VMEM((8, LANES), f32)),
        [
            pltpu.VMEM((TS, TS, TS), f32),
            pltpu.VMEM((TS, TS, TS), jnp.int32),
            pltpu.VMEM(right.shape, bf16),
            pltpu.VMEM(small.shape, f32),
            pltpu.SemaphoreType.DMA((4,)),
        ],
        (templates[0], wedge, right, small), [HBM] * 4, 1 << 22, 1 << 20, None,
    )
    other = swap(normed, 4)
    window = call(
        window_kernel, pltpu.VMEM((NF, SLAB, NY), f32),
        [pltpu.VMEM((NY // LANES, SLAB, NF, LANES), f32), pltpu.SemaphoreType.DMA((8,))],
        (token, volume), [VMEM, HBM], 1 << 31, 1 << 19, 16 * 1024 * 1024,
    )
    fan = call(
        fan_kernel, pltpu.VMEM((8, 2 * TS, TS * TS), f32), [], (normed, other), [VMEM] * 2, 1 << 33, 1 << 18
    )
    near = [[8 * a + b for a in range(8)] for b in range(8)]
    gathered = lax.all_to_all(
        fan, "orient", 0, 0, tiled=True, axis_index_groups=near
    ).reshape(NO * TS, TS * TS)

    slabs = lax.axis_size("zslab")
    inside = lax.ppermute(window, "zslab", [(s, s ^ 1) for s in range(slabs)])
    across = lax.ppermute(window, "zslab", [(1, 2), (2, 1)])
    inside, gathered = lax.optimization_barrier((inside, gathered))
    spectrum = jax.ShapeDtypeStruct((NK, 128, NY), bf16)
    high, low = call(
        volume_kernel, (spectrum, spectrum), [pltpu.VMEM((NK, 48, NY), f32)],
        (inside, window, across), [VMEM] * 3, 1 << 24, 1 << 21,
    )
    spread = jnp.asarray(spread_table(), bf16)
    strip = jax.ShapeDtypeStruct((STRIP, SLAB, NY), f32)
    parts = call(
        score_kernel, (strip,) * 4,
        [
            pltpu.VMEM((KDIM // 2 // LANES, NO * TS, LANES), f32),
            pltpu.VMEM((NK, 2, 2, NO, KDIM // 2), bf16),
            pltpu.VMEM((512, KDIM), bf16),
            pltpu.VMEM((512, KDIM), bf16),
            pltpu.VMEM((KDIM, NY), bf16),
            pltpu.VMEM((KDIM, NY), bf16),
            pltpu.VMEM((KDIM, NY), bf16),
            pltpu.VMEM((KDIM, NY), bf16),
            pltpu.VMEM((4, 256, NY), f32),
            pltpu.VMEM((4, 256, NY), f32),
            pltpu.VMEM((4, 4, 2, 128, NY), f32),
            pltpu.VMEM((NF // 2, SLAB, NY), f32),
        ],
        (gathered, spread, high, low), [VMEM] * 4, 1 << 33, 1 << 21,
    )
    late, _ = lax.optimization_barrier((inside, parts[1]))
    scale = call(
        scale_kernel, strip, [], (late, window, across), [VMEM] * 3, 1 << 22, 1 << 20
    )
    arrived = [parts[0]] + [swap(parts[m], m) for m in range(1, GROUP)]
    return call(
        last_kernel, jax.ShapeDtypeStruct((SLAB, STRIP, NY), f32), [],
        (scale, *arrived), [VMEM] * 5, 1 << 16, 1 << 18,
    )


def solution(mesh):
    return jax.shard_map(
        shards,
        mesh=mesh,
        in_specs=(P("zslab", None, None), P("orient", None, None, None), P()),
        out_specs=P("zslab", "orient", None),
        check_vma=False,
    )
```

```python
import math

import jax
import jax.numpy as jnp
import numpy as np
from jax import lax
from jax.experimental import pallas as pl
from jax.experimental.pallas import tpu as pltpu
from jax.sharding import PartitionSpec as P

TS = 16
HALF = 8
NF = 32
NK = 16
SLAB = 8
NY = 256
GROUP = 4
NO = 16
STRIP = 4
LANES = 128
KDIM = TS * 48
EXACT = lax.Precision.HIGHEST
VMEM = pl.BlockSpec(memory_space=pltpu.VMEM)
HBM = pl.BlockSpec(memory_space=pltpu.HBM)


def plus(a, b):
    if a is None:
        return b
    return a if b is None else a + b


def minus(a, b):
    if b is None:
        return a
    return -b if a is None else a - b


def twiddled(value, k, count, sign):
    re, im = value
    if k == 0:
        return value
    if 4 * k == count:
        return (None if im is None else -sign * im, None if re is None else sign * re)
    c = math.cos(2.0 * math.pi * k / count)
    s = sign * math.sin(2.0 * math.pi * k / count)
    if im is None:
        return (c * re, s * re)
    if re is None:
        return (-s * im, c * im)
    return (c * re - s * im, s * re + c * im)


def forward(rows):
    count = len(rows)
    if count == 2:
        return [(plus(rows[0], rows[1]), None), (minus(rows[0], rows[1]), None)]
    even, odd = forward(rows[::2]), forward(rows[1::2])
    bins = [None] * (count // 2 + 1)
    for k in range(count // 4 + 1):
        e, o = even[k], twiddled(odd[k], k, count, -1.0)
        bins[k] = (plus(e[0], o[0]), plus(e[1], o[1]))
        if 4 * k != count:
            re, im = minus(e[0], o[0]), minus(e[1], o[1])
            bins[count // 2 - k] = (re, None if im is None else -im)
    return bins


def inverse_step(bins, count):
    even, odd = {}, {}
    for k in range(count // 4 + 1):
        if k not in bins:
            continue
        a, b = bins[k], bins[count // 2 - k]
        if k == 0:
            even[k] = (a[0] + b[0], None)
            odd[k] = (a[0] - b[0], None)
        elif 4 * k == count:
            even[k] = (2.0 * a[0], None)
            odd[k] = (-2.0 * a[1], None)
        else:
            even[k] = (a[0] + b[0], a[1] - b[1])
            odd[k] = twiddled((a[0] - b[0], a[1] + b[1]), k, count, 1.0)
    return even, odd


def inverse(bins, count, need):
    if count == 2:
        first = bins[0][0] + bins[1][0]
        return [first] if need == 1 else [first, bins[0][0] - bins[1][0]]
    even, odd = inverse_step(bins, count)
    rows = [None] * need
    rows[::2] = inverse(even, count // 2, (need + 1) // 2)
    rows[1::2] = inverse(odd, count // 2, need // 2)
    return rows


def slots(bins):
    return [(bins[0][0], bins[NK][0])] + [bins[k] for k in range(1, NK)]


QUADS = ((0, 4, 8, 12), (1, 7, 9, 15), (2, 6, 10, 14), (3, 5, 11, 13))


def halves(value):
    high = value.astype(jnp.bfloat16)
    return high, (value - high.astype(jnp.float32)).astype(jnp.bfloat16)


def two_terms(table):
    high = np.asarray(table, jnp.bfloat16)
    return np.stack([high, np.asarray(table - high.astype(np.float64), jnp.bfloat16)])


def filter_tables():
    small = np.arange(TS)
    pair = 2.0 * math.pi * np.outer(small, small) / TS
    two = pair[:, None, :, None] + pair[None, :, None, :]
    two = two.reshape(TS * TS, TS * TS)
    right = np.concatenate([np.cos(two), -np.sin(two)], axis=1)
    c, s = np.cos(pair), np.sin(pair)
    ahead = np.block([[c, s], [-s, c]])
    back = np.block([[c, -s], [s, c]])
    return two_terms(right), np.float32(np.stack([ahead, back]))


def spread_table():
    out = np.zeros((TS, TS, TS, 24), np.float32)
    for b in range(TS):
        for c in range(TS):
            out[c, b, b, c] = 1.0
    return out.reshape(TS * TS, KDIM // 2)


def front_kernel(
    template_hbm, wedge_hbm, volume_hbm, right_hbm, small_hbm, out_ref, window_ref,
    template_ref, wedge_ref, right_ref, small_ref, piece_ref, sems,
):
    width = TS * TS
    copies = [
        pltpu.make_async_copy(src, dst, sems.at[i])
        for i, (src, dst) in enumerate(
            ((template_hbm, template_ref), (right_hbm, right_ref), (small_hbm, small_ref), (wedge_hbm, wedge_ref))
        )
    ]
    for copy in copies:
        copy.start()
    rows = volume_hbm.shape[1]
    first = lax.axis_index("orient") // GROUP * 16 + (rows - HALF)
    pieces = []
    for j in range(NF // 8):
        at = pl.multiple_of(lax.rem(first + 8 * j, rows), 8)
        for h in range(NY // LANES):
            copy = pltpu.make_async_copy(
                volume_hbm.at[:, pl.ds(at, 8), pl.ds(h * LANES, LANES)],
                piece_ref.at[h, :, pl.ds(8 * j, 8), :],
                sems.at[4 + len(pieces)],
            )
            copy.start()
            pieces.append(copy)

    def flat(ref):
        return jnp.concatenate([ref[c].astype(jnp.float32) for c in range(TS)], axis=1)

    def exact(a, b):
        return jnp.dot(a, b, precision=EXACT, preferred_element_type=jnp.float32)

    def product(value, lanes):
        rows = value.shape[0]
        both = jnp.concatenate(halves(value), axis=0)
        out = jnp.dot(both, right_ref[0, :, lanes], preferred_element_type=jnp.float32)
        low = jnp.dot(both[:rows], right_ref[1, :, lanes], preferred_element_type=jnp.float32)
        return out[:rows] + (out[rows:] + low)

    for copy in copies:
        copy.wait()
    spec = product(flat(template_ref), slice(0, 2 * width))
    spec = jnp.concatenate([spec[:, :width], spec[:, width:]], axis=0)
    keep = flat(wedge_ref)
    spec = exact(small_ref[0], spec) * jnp.concatenate([keep, keep], axis=0)
    spec = exact(small_ref[1], spec)
    filt = product(spec[:TS], slice(0, width)) + product(spec[TS:], slice(width, 2 * width))
    filt = filt * (1.0 / float(TS**3))
    centered = filt - jnp.sum(filt) * (1.0 / float(TS**3))
    out_ref[...] = centered / jnp.sqrt(jnp.sum(centered * centered) + 1e-05)
    for copy in pieces:
        copy.wait()
    flat_piece = piece_ref.reshape(NY // LANES, SLAB * NF, LANES)
    for h in range(NY // LANES):
        for x in range(NF):
            window_ref[x, :, h * LANES : (h + 1) * LANES] = flat_piece[h, pl.ds(x, SLAB, stride=NF), :]


def fan_kernel(own_ref, other_ref, out_ref):
    own, other = own_ref[...], other_ref[...]
    for i in range(out_ref.shape[0]):
        out_ref[i, :TS], out_ref[i, TS:] = own, other


def volume_kernel(inside_ref, own_ref, across_ref, high_ref, low_ref, spec_ref):
    even = lax.rem(lax.axis_index("zslab"), 2) == 0
    inside_at = pl.multiple_of(jnp.where(even, 16, 0), 8)
    across_at = pl.multiple_of(16 - inside_at, 8)
    for ref, start in ((inside_ref, inside_at), (own_ref, 8), (across_ref, across_at)):
        for lane in range(0, NY, LANES):
            bins = forward([ref[x, :, lane : lane + LANES] for x in range(NF)])
            for k, (re, im) in enumerate(slots(bins)):
                spec_ref[k, pl.ds(start, 8), lane : lane + LANES] = re
                spec_ref[k, pl.ds(start + 24, 8), lane : lane + LANES] = im

    def split(k, carry):
        nil = jnp.zeros((8, NY), jnp.float32)
        for part in range(2):
            a, b, c = (spec_ref[k, 24 * part + 8 * j : 24 * part + 8 * j + 8, :] for j in range(3))
            rows = slice(64 * part, 64 * part + 64)
            high_ref[k, rows], low_ref[k, rows] = halves(
                jnp.concatenate([a, b, c, nil, nil, a, b, c], axis=0)
            )
        return carry

    lax.fori_loop(0, NK, split, 0)


def scale_kernel(inside_ref, own_ref, across_ref, scale_ref):
    even = lax.rem(lax.axis_index("zslab"), 2) == 0
    first = lax.rem(lax.axis_index("orient"), GROUP) * STRIP
    sums = []
    for x in range(STRIP + TS - 1):
        inside, across = inside_ref[first + x], across_ref[first + x]
        layers = jnp.concatenate(
            [jnp.where(even, across, inside), own_ref[first + x], jnp.where(even, inside, across)], axis=0
        )
        sums.append(layers * layers)
    for step in (1, 2, 4, 8):
        sums = [sums[i] + sums[i + step] for i in range(len(sums) - step)]
    for x in range(STRIP):
        total = sums[x]
        for step in (1, 2, 4, 8):
            total = total + pltpu.roll(total, 24 - step, axis=0)
        total = total[:SLAB]
        for step in (1, 2, 4, 8):
            total = total + pltpu.roll(total, NY - step, axis=1)
        total = pltpu.roll(total, HALF, axis=1)
        scale_ref[x] = (1.0 / NF) / jnp.sqrt(total * (1.0 / float(TS**3)) + 1e-05)


def score_kernel(
    gathered_ref, spread_ref, high_ref, low_ref,
    out0_ref, out1_ref, out2_ref, out3_ref,
    wide_ref, base_ref, left_a, left_b, high_a, high_b, low_a, low_b, prod_a, prod_b, part_ref, best_ref,
):
    side = KDIM // 2
    high, low = halves(gathered_ref[...])
    wide = jnp.dot(high, spread_ref[...], preferred_element_type=jnp.float32) + jnp.dot(
        low, spread_ref[...], preferred_element_type=jnp.float32
    )
    for j in range(side // LANES):
        wide_ref[j] = wide[:, j * LANES : (j + 1) * LANES]
    for j in range(side // LANES):
        groups = []
        for o in (0, 8):
            rows = [wide_ref[j, pl.ds(o * TS + a, 8, stride=TS), :] for a in range(TS)]
            groups.append(slots(forward(rows + [None] * (NF - TS))))
        for k, ((re0, im0), (re1, im1)) in enumerate(zip(*groups)):
            re = halves(jnp.concatenate([re0, re1], axis=0))
            im = halves(jnp.concatenate([im0, im1], axis=0))
            for h in range(2):
                base_ref[k, h, 0, :, j * LANES : (j + 1) * LANES] = re[h]
                base_ref[k, h, 1, :, j * LANES : (j + 1) * LANES] = im[h]

    def turned(value, shift, axis=1):
        shift = shift % value.shape[axis]
        return value if shift == 0 else pltpu.roll(value, shift, axis=axis)

    def build(k, left, right_high, right_low):
        for h in range(2):
            re, im = base_ref[k, h, 0], base_ref[k, h, 1]
            for z in range(SLAB):
                row = h * 256 + z * NO
                rows, more = slice(row, row + NO), slice(row + 128, row + 128 + NO)
                re_z, im_z = turned(re, z), turned(im, z)
                left[rows, :side] = re_z
                if k == 0:
                    nil = jnp.zeros_like(re_z)
                    left[rows, side:] = nil
                    left[more, :side] = nil
                    left[more, side:] = im_z
                else:
                    left[rows, side:] = im_z
                    left[more, :side] = -im_z
                    left[more, side:] = re_z
        for src, dst in ((high_ref, right_high), (low_ref, right_low)):
            for part in range(2):
                a, b, c, d = (src[k, 64 * part + 16 * j : 64 * part + 16 * j + 16, :] for j in range(4))
                for y in range(0, TS, 2):
                    row = side * part + 24 * y
                    here, after = HALF - y, HALF - y - 1
                    dst[row : row + 16, :] = turned(a, here)
                    dst[row + 16 : row + 32, :] = turned(b, here) + turned(c, after)
                    dst[row + 32 : row + 48, :] = turned(d, after)

    def multiply(prod, left, right_high, right_low):
        both = jnp.dot(left[...], right_high[...], preferred_element_type=jnp.float32)
        low = jnp.dot(left[:256], right_low[...], preferred_element_type=jnp.float32)
        prod[...] = both[:256] + (both[256:] + low)

    def combine(quad, prod, groups):
        for group in groups:
            row, lane = group // 2 * 8, group % 2 * LANES
            bins = {}
            for j, k in enumerate(QUADS[quad]):
                re, im = (prod[j, r : r + 8, lane : lane + LANES] for r in (row, 128 + row))
                if k == 0:
                    bins[0], bins[NK] = (re, None), (im, None)
                else:
                    bins[k] = (re, im)
            for i, one in enumerate(inverse_step(bins, NF)):
                for j, two in enumerate(inverse_step(one, NF // 2)):
                    pair = (two[0][0], two[4][0]) if quad == 0 else two[quad]
                    for part in range(2):
                        part_ref[quad, i + 2 * j, part, row : row + 8, lane : lane + LANES] = pair[part]

    order = [k for quad in QUADS for k in quad]
    slot = ((left_a, high_a, low_a), (left_b, high_b, low_b))
    prods = (prod_a, prod_b)
    build(order[0], *slot[0])
    for i in range(NK):
        multiply(prods[i // 4 % 2].at[i % 4], *slot[i % 2])
        if i + 1 < NK:
            build(order[i + 1], *slot[(i + 1) % 2])
        if i >= 4:
            combine(i // 4 - 1, prods[(i // 4 - 1) % 2], range(8 * (i % 4), 8 * (i % 4) + 8))
    combine(3, prods[1], range(32))
    best_ref[...] = jnp.zeros_like(best_ref)

    def finish(z, carry):
        row = pl.multiple_of(z * NO, NO)
        here = lax.broadcasted_iota(jnp.int32, (SLAB, LANES), 0) == z
        for lane in range(0, NY, LANES):
            for sub in range(4):
                top = None
                for o in (0, 8):
                    pairs = [
                        tuple(part_ref[q, sub, p, pl.ds(row + o, 8), lane : lane + LANES] for p in range(2))
                        for q in range(4)
                    ]
                    bins = {0: (pairs[0][0], None), 4: (pairs[0][1], None)}
                    bins.update({q: pairs[q] for q in range(1, 4)})
                    rows = inverse(bins, 8, 4)
                    top = rows if top is None else [jnp.maximum(a, b) for a, b in zip(top, rows)]
                for m in range(4):
                    x = 4 * m + sub
                    largest = jnp.max(top[m], axis=0, keepdims=True)
                    best_ref[x, :, lane : lane + LANES] = jnp.where(
                        here, largest, best_ref[x, :, lane : lane + LANES]
                    )
        return carry

    lax.fori_loop(0, SLAB, finish, 0)
    mine = lax.rem(lax.axis_index("orient"), GROUP)
    for m, ref in enumerate((out0_ref, out1_ref, out2_ref, out3_ref)):
        ref[...] = best_ref[pl.ds((mine ^ m) * STRIP, STRIP)]


def last_kernel(scale_ref, a_ref, b_ref, c_ref, d_ref, out_ref):
    for x in range(STRIP):
        top = jnp.maximum(jnp.maximum(a_ref[x], b_ref[x]), jnp.maximum(c_ref[x], d_ref[x]))
        out_ref[:, x, :] = top * scale_ref[x]


def call(kernel, outs, scratch, args, specs, flops=0, nbytes=0, limit=48 * 1024 * 1024):
    return pl.pallas_call(
        kernel,
        out_shape=outs,
        in_specs=specs,
        out_specs=[VMEM] * len(outs) if isinstance(outs, (list, tuple)) else VMEM,
        scratch_shapes=scratch,
        compiler_params=pltpu.CompilerParams(vmem_limit_bytes=limit),
        cost_estimate=pl.CostEstimate(flops=flops, bytes_accessed=nbytes, transcendentals=0),
    )(*args)


def shards(volume, templates, wedge):
    f32, bf16 = jnp.float32, jnp.bfloat16
    count = lax.axis_size("orient")
    def swap(value, mask):
        return lax.ppermute(value, "orient", [(i, i ^ mask) for i in range(count)])

    right, small = (jnp.asarray(t) for t in filter_tables())
    normed, window = call(
        front_kernel,
        (pltpu.VMEM((TS, TS * TS), f32), pltpu.VMEM((NF, SLAB, NY), f32)),
        [
            pltpu.VMEM((TS, TS, TS), f32),
            pltpu.VMEM((TS, TS, TS), jnp.int32),
            pltpu.VMEM(right.shape, bf16),
            pltpu.VMEM(small.shape, f32),
            pltpu.VMEM((NY // LANES, SLAB, NF, LANES), f32),
            pltpu.SemaphoreType.DMA((12,)),
        ],
        (templates[0], wedge, volume, right, small), [HBM] * 5, 1 << 22, 1 << 20, None,
    )
    other = swap(normed, 4)
    fan = call(
        fan_kernel, pltpu.VMEM((8, 2 * TS, TS * TS), f32), [], (normed, other), [VMEM] * 2, 1 << 33, 1 << 18
    )
    near = [[8 * a + b for a in range(8)] for b in range(8)]
    gathered = lax.all_to_all(
        fan, "orient", 0, 0, tiled=True, axis_index_groups=near
    ).reshape(NO * TS, TS * TS)

    slabs = lax.axis_size("zslab")
    inside = lax.ppermute(window, "zslab", [(s, s ^ 1) for s in range(slabs)])
    later, inside = lax.optimization_barrier((window, inside))
    across = lax.ppermute(later, "zslab", [(1, 2), (2, 1)])
    inside, gathered = lax.optimization_barrier((inside, gathered))
    spectrum = jax.ShapeDtypeStruct((NK, 128, NY), bf16)
    high, low = call(
        volume_kernel, (spectrum, spectrum), [pltpu.VMEM((NK, 48, NY), f32)],
        (inside, window, across), [VMEM] * 3, 1 << 24, 1 << 21,
    )
    spread = jnp.asarray(spread_table(), bf16)
    strip = jax.ShapeDtypeStruct((STRIP, SLAB, NY), f32)
    parts = call(
        score_kernel, (strip,) * 4,
        [
            pltpu.VMEM((KDIM // 2 // LANES, NO * TS, LANES), f32),
            pltpu.VMEM((NK, 2, 2, NO, KDIM // 2), bf16),
            pltpu.VMEM((512, KDIM), bf16),
            pltpu.VMEM((512, KDIM), bf16),
            pltpu.VMEM((KDIM, NY), bf16),
            pltpu.VMEM((KDIM, NY), bf16),
            pltpu.VMEM((KDIM, NY), bf16),
            pltpu.VMEM((KDIM, NY), bf16),
            pltpu.VMEM((4, 256, NY), f32),
            pltpu.VMEM((4, 256, NY), f32),
            pltpu.VMEM((4, 4, 2, 128, NY), f32),
            pltpu.VMEM((NF // 2, SLAB, NY), f32),
        ],
        (gathered, spread, high, low), [VMEM] * 4, 1 << 33, 1 << 21,
    )
    late, _ = lax.optimization_barrier((inside, parts[1]))
    scale = call(
        scale_kernel, strip, [], (late, window, across), [VMEM] * 3, 1 << 22, 1 << 20
    )
    arrived = [parts[0]] + [swap(parts[m], m) for m in range(1, GROUP)]
    return call(
        last_kernel, jax.ShapeDtypeStruct((SLAB, STRIP, NY), f32), [],
        (scale, *arrived), [VMEM] * 5, 1 << 16, 1 << 18,
    )


def solution(mesh):
    return jax.shard_map(
        shards,
        mesh=mesh,
        in_specs=(P("zslab", None, None), P("orient", None, None, None), P()),
        out_specs=P("zslab", "orient", None),
        check_vma=False,
    )
```

```python
import math

import jax
import jax.numpy as jnp
import numpy as np
from jax import lax
from jax.experimental import pallas as pl
from jax.experimental.pallas import tpu as pltpu
from jax.sharding import PartitionSpec as P

TS = 16
HALF = 8
NF = 32
NK = 16
SLAB = 8
NY = 256
GROUP = 4
NO = 16
STRIP = 4
LANES = 128
KDIM = TS * 48
EXACT = lax.Precision.HIGHEST
VMEM = pl.BlockSpec(memory_space=pltpu.VMEM)
HBM = pl.BlockSpec(memory_space=pltpu.HBM)


def plus(a, b):
    if a is None:
        return b
    return a if b is None else a + b


def minus(a, b):
    if b is None:
        return a
    return -b if a is None else a - b


def twiddled(value, k, count, sign):
    re, im = value
    if k == 0:
        return value
    if 4 * k == count:
        return (None if im is None else -sign * im, None if re is None else sign * re)
    c = math.cos(2.0 * math.pi * k / count)
    s = sign * math.sin(2.0 * math.pi * k / count)
    if im is None:
        return (c * re, s * re)
    if re is None:
        return (-s * im, c * im)
    return (c * re - s * im, s * re + c * im)


def forward(rows):
    count = len(rows)
    if count == 2:
        return [(plus(rows[0], rows[1]), None), (minus(rows[0], rows[1]), None)]
    even, odd = forward(rows[::2]), forward(rows[1::2])
    bins = [None] * (count // 2 + 1)
    for k in range(count // 4 + 1):
        e, o = even[k], twiddled(odd[k], k, count, -1.0)
        bins[k] = (plus(e[0], o[0]), plus(e[1], o[1]))
        if 4 * k != count:
            re, im = minus(e[0], o[0]), minus(e[1], o[1])
            bins[count // 2 - k] = (re, None if im is None else -im)
    return bins


def inverse_step(bins, count):
    even, odd = {}, {}
    for k in range(count // 4 + 1):
        if k not in bins:
            continue
        a, b = bins[k], bins[count // 2 - k]
        if k == 0:
            even[k] = (a[0] + b[0], None)
            odd[k] = (a[0] - b[0], None)
        elif 4 * k == count:
            even[k] = (2.0 * a[0], None)
            odd[k] = (-2.0 * a[1], None)
        else:
            even[k] = (a[0] + b[0], a[1] - b[1])
            odd[k] = twiddled((a[0] - b[0], a[1] + b[1]), k, count, 1.0)
    return even, odd


def inverse(bins, count, need):
    if count == 2:
        first = bins[0][0] + bins[1][0]
        return [first] if need == 1 else [first, bins[0][0] - bins[1][0]]
    even, odd = inverse_step(bins, count)
    rows = [None] * need
    rows[::2] = inverse(even, count // 2, (need + 1) // 2)
    rows[1::2] = inverse(odd, count // 2, need // 2)
    return rows


def slots(bins):
    return [(bins[0][0], bins[NK][0])] + [bins[k] for k in range(1, NK)]


QUADS = ((0, 4, 8, 12), (1, 7, 9, 15), (2, 6, 10, 14), (3, 5, 11, 13))


def halves(value):
    high = value.astype(jnp.bfloat16)
    return high, (value - high.astype(jnp.float32)).astype(jnp.bfloat16)


def two_terms(table):
    high = np.asarray(table, jnp.bfloat16)
    return np.stack([high, np.asarray(table - high.astype(np.float64), jnp.bfloat16)])


def filter_tables():
    small = np.arange(TS)
    pair = 2.0 * math.pi * np.outer(small, small) / TS
    two = pair[:, None, :, None] + pair[None, :, None, :]
    two = two.reshape(TS * TS, TS * TS)
    right = np.concatenate([np.cos(two), -np.sin(two)], axis=1)
    c, s = np.cos(pair), np.sin(pair)
    ahead = np.block([[c, s], [-s, c]])
    back = np.block([[c, -s], [s, c]])
    return two_terms(right), np.float32(np.stack([ahead, back]))


def spread_table():
    out = np.zeros((TS, TS, TS, 24), np.float32)
    for b in range(TS):
        for c in range(TS):
            out[c, b, b, c] = 1.0
    return out.reshape(TS * TS, KDIM // 2)


def front_kernel(
    template_hbm, wedge_hbm, volume_hbm, right_hbm, small_hbm, out_ref, window_ref,
    template_ref, wedge_ref, right_ref, small_ref, piece_ref, sems,
):
    width = TS * TS
    copies = [
        pltpu.make_async_copy(src, dst, sems.at[i])
        for i, (src, dst) in enumerate(
            ((template_hbm, template_ref), (right_hbm, right_ref), (small_hbm, small_ref), (wedge_hbm, wedge_ref))
        )
    ]
    for copy in copies:
        copy.start()
    rows = volume_hbm.shape[1]
    first = lax.axis_index("orient") // GROUP * 16 + (rows - HALF)
    pieces = []
    for j in range(NF // 8):
        at = pl.multiple_of(lax.rem(first + 8 * j, rows), 8)
        for h in range(NY // LANES):
            copy = pltpu.make_async_copy(
                volume_hbm.at[:, pl.ds(at, 8), pl.ds(h * LANES, LANES)],
                piece_ref.at[h, :, pl.ds(8 * j, 8), :],
                sems.at[4 + len(pieces)],
            )
            copy.start()
            pieces.append(copy)

    def flat(ref):
        return jnp.concatenate([ref[c].astype(jnp.float32) for c in range(TS)], axis=1)

    def exact(a, b):
        return jnp.dot(a, b, precision=EXACT, preferred_element_type=jnp.float32)

    def product(value, lanes):
        rows = value.shape[0]
        both = jnp.concatenate(halves(value), axis=0)
        out = jnp.dot(both, right_ref[0, :, lanes], preferred_element_type=jnp.float32)
        low = jnp.dot(both[:rows], right_ref[1, :, lanes], preferred_element_type=jnp.float32)
        return out[:rows] + (out[rows:] + low)

    for copy in copies:
        copy.wait()
    spec = product(flat(template_ref), slice(0, 2 * width))
    spec = jnp.concatenate([spec[:, :width], spec[:, width:]], axis=0)
    keep = flat(wedge_ref)
    spec = exact(small_ref[0], spec) * jnp.concatenate([keep, keep], axis=0)
    spec = exact(small_ref[1], spec)
    filt = product(spec[:TS], slice(0, width)) + product(spec[TS:], slice(width, 2 * width))
    filt = filt * (1.0 / float(TS**3))
    centered = filt - jnp.sum(filt) * (1.0 / float(TS**3))
    out_ref[...] = centered / jnp.sqrt(jnp.sum(centered * centered) + 1e-05)
    for copy in pieces:
        copy.wait()
    flat_piece = piece_ref.reshape(NY // LANES, SLAB * NF, LANES)
    for h in range(NY // LANES):
        for x in range(NF):
            window_ref[x, :, h * LANES : (h + 1) * LANES] = flat_piece[h, pl.ds(x, SLAB, stride=NF), :]


def fan_kernel(own_ref, other_ref, out_ref):
    own, other = own_ref[...], other_ref[...]
    for i in range(out_ref.shape[0]):
        out_ref[i, :TS], out_ref[i, TS:] = own, other


def volume_kernel(inside_ref, own_ref, across_ref, high_ref, low_ref, spec_ref):
    even = lax.rem(lax.axis_index("zslab"), 2) == 0
    inside_at = pl.multiple_of(jnp.where(even, 16, 0), 8)
    across_at = pl.multiple_of(16 - inside_at, 8)
    for ref, start in ((inside_ref, inside_at), (own_ref, 8), (across_ref, across_at)):
        for lane in range(0, NY, LANES):
            bins = forward([ref[x, :, lane : lane + LANES] for x in range(NF)])
            for k, (re, im) in enumerate(slots(bins)):
                spec_ref[k, pl.ds(start, 8), lane : lane + LANES] = re
                spec_ref[k, pl.ds(start + 24, 8), lane : lane + LANES] = im

    def split(k, carry):
        nil = jnp.zeros((8, NY), jnp.float32)
        for part in range(2):
            a, b, c = (spec_ref[k, 24 * part + 8 * j : 24 * part + 8 * j + 8, :] for j in range(3))
            rows = slice(64 * part, 64 * part + 64)
            high_ref[k, rows], low_ref[k, rows] = halves(
                jnp.concatenate([a, b, c, nil, nil, a, b, c], axis=0)
            )
        return carry

    lax.fori_loop(0, NK, split, 0, unroll=4)


def scale_kernel(inside_ref, own_ref, across_ref, scale_ref):
    even = lax.rem(lax.axis_index("zslab"), 2) == 0
    first = lax.rem(lax.axis_index("orient"), GROUP) * STRIP
    sums = []
    for x in range(STRIP + TS - 1):
        inside, across = inside_ref[first + x], across_ref[first + x]
        layers = jnp.concatenate(
            [jnp.where(even, across, inside), own_ref[first + x], jnp.where(even, inside, across)], axis=0
        )
        sums.append(layers * layers)
    for step in (1, 2, 4, 8):
        sums = [sums[i] + sums[i + step] for i in range(len(sums) - step)]
    for x in range(STRIP):
        total = sums[x]
        for step in (1, 2, 4, 8):
            total = total + pltpu.roll(total, 24 - step, axis=0)
        total = total[:SLAB]
        for step in (1, 2, 4, 8):
            total = total + pltpu.roll(total, NY - step, axis=1)
        total = pltpu.roll(total, HALF, axis=1)
        scale_ref[x] = (1.0 / NF) / jnp.sqrt(total * (1.0 / float(TS**3)) + 1e-05)


def score_kernel(
    gathered_ref, spread_ref, high_ref, low_ref,
    out0_ref, out1_ref, out2_ref, out3_ref,
    wide_ref, base_ref, left_a, left_b, high_a, high_b, low_a, low_b, prod_a, prod_b, part_ref, best_ref,
):
    side = KDIM // 2
    high, low = halves(gathered_ref[...])
    wide = jnp.dot(high, spread_ref[...], preferred_element_type=jnp.float32) + jnp.dot(
        low, spread_ref[...], preferred_element_type=jnp.float32
    )
    for j in range(side // LANES):
        wide_ref[j] = wide[:, j * LANES : (j + 1) * LANES]
    for j in range(side // LANES):
        groups = []
        for o in (0, 8):
            rows = [wide_ref[j, pl.ds(o * TS + a, 8, stride=TS), :] for a in range(TS)]
            groups.append(slots(forward(rows + [None] * (NF - TS))))
        for k, ((re0, im0), (re1, im1)) in enumerate(zip(*groups)):
            re = halves(jnp.concatenate([re0, re1], axis=0))
            im = halves(jnp.concatenate([im0, im1], axis=0))
            for h in range(2):
                base_ref[k, h, 0, :, j * LANES : (j + 1) * LANES] = re[h]
                base_ref[k, h, 1, :, j * LANES : (j + 1) * LANES] = im[h]

    def turned(value, shift, axis=1):
        shift = shift % value.shape[axis]
        return value if shift == 0 else pltpu.roll(value, shift, axis=axis)

    def build(k, left, right_high, right_low):
        for h in range(2):
            re, im = base_ref[k, h, 0], base_ref[k, h, 1]
            for z in range(SLAB):
                row = h * 256 + z * NO
                rows, more = slice(row, row + NO), slice(row + 128, row + 128 + NO)
                re_z, im_z = turned(re, z), turned(im, z)
                left[rows, :side] = re_z
                if k == 0:
                    nil = jnp.zeros_like(re_z)
                    left[rows, side:] = nil
                    left[more, :side] = nil
                    left[more, side:] = im_z
                else:
                    left[rows, side:] = im_z
                    left[more, :side] = -im_z
                    left[more, side:] = re_z
        for src, dst in ((high_ref, right_high), (low_ref, right_low)):
            for part in range(2):
                a, b, c, d = (src[k, 64 * part + 16 * j : 64 * part + 16 * j + 16, :] for j in range(4))
                for y in range(0, TS, 2):
                    row = side * part + 24 * y
                    here, after = HALF - y, HALF - y - 1
                    dst[row : row + 16, :] = turned(a, here)
                    dst[row + 16 : row + 32, :] = turned(b, here) + turned(c, after)
                    dst[row + 32 : row + 48, :] = turned(d, after)

    def multiply(prod, left, right_high, right_low):
        both = jnp.dot(left[...], right_high[...], preferred_element_type=jnp.float32)
        low = jnp.dot(left[:256], right_low[...], preferred_element_type=jnp.float32)
        prod[...] = both[:256] + (both[256:] + low)

    def combine(quad, prod, groups):
        for group in groups:
            row, lane = group // 2 * 8, group % 2 * LANES
            bins = {}
            for j, k in enumerate(QUADS[quad]):
                re, im = (prod[j, r : r + 8, lane : lane + LANES] for r in (row, 128 + row))
                if k == 0:
                    bins[0], bins[NK] = (re, None), (im, None)
                else:
                    bins[k] = (re, im)
            for i, one in enumerate(inverse_step(bins, NF)):
                for j, two in enumerate(inverse_step(one, NF // 2)):
                    pair = (two[0][0], two[4][0]) if quad == 0 else two[quad]
                    for part in range(2):
                        part_ref[quad, i + 2 * j, part, row : row + 8, lane : lane + LANES] = pair[part]

    order = [k for quad in QUADS for k in quad]
    slot = ((left_a, high_a, low_a), (left_b, high_b, low_b))
    prods = (prod_a, prod_b)
    build(order[0], *slot[0])
    for i in range(NK):
        multiply(prods[i // 4 % 2].at[i % 4], *slot[i % 2])
        if i + 1 < NK:
            build(order[i + 1], *slot[(i + 1) % 2])
        if i >= 4:
            combine(i // 4 - 1, prods[(i // 4 - 1) % 2], range(8 * (i % 4), 8 * (i % 4) + 8))
    combine(3, prods[1], range(32))
    best_ref[...] = jnp.zeros_like(best_ref)

    def finish(z, carry):
        row = pl.multiple_of(z * NO, NO)
        here = lax.broadcasted_iota(jnp.int32, (SLAB, LANES), 0) == z
        for lane in range(0, NY, LANES):
            for sub in range(4):
                top = None
                for o in (0, 8):
                    pairs = [
                        tuple(part_ref[q, sub, p, pl.ds(row + o, 8), lane : lane + LANES] for p in range(2))
                        for q in range(4)
                    ]
                    bins = {0: (pairs[0][0], None), 4: (pairs[0][1], None)}
                    bins.update({q: pairs[q] for q in range(1, 4)})
                    rows = inverse(bins, 8, 4)
                    top = rows if top is None else [jnp.maximum(a, b) for a, b in zip(top, rows)]
                for m in range(4):
                    x = 4 * m + sub
                    largest = jnp.max(top[m], axis=0, keepdims=True)
                    best_ref[x, :, lane : lane + LANES] = jnp.where(
                        here, largest, best_ref[x, :, lane : lane + LANES]
                    )
        return carry

    lax.fori_loop(0, SLAB, finish, 0, unroll=2)
    mine = lax.rem(lax.axis_index("orient"), GROUP)
    for m, ref in enumerate((out0_ref, out1_ref, out2_ref, out3_ref)):
        ref[...] = best_ref[pl.ds((mine ^ m) * STRIP, STRIP)]


def last_kernel(scale_ref, a_ref, b_ref, c_ref, d_ref, out_ref):
    for x in range(STRIP):
        top = jnp.maximum(jnp.maximum(a_ref[x], b_ref[x]), jnp.maximum(c_ref[x], d_ref[x]))
        out_ref[:, x, :] = top * scale_ref[x]


def call(kernel, outs, scratch, args, specs, flops=0, nbytes=0, limit=48 * 1024 * 1024):
    return pl.pallas_call(
        kernel,
        out_shape=outs,
        in_specs=specs,
        out_specs=[VMEM] * len(outs) if isinstance(outs, (list, tuple)) else VMEM,
        scratch_shapes=scratch,
        compiler_params=pltpu.CompilerParams(vmem_limit_bytes=limit),
        cost_estimate=pl.CostEstimate(flops=flops, bytes_accessed=nbytes, transcendentals=0),
    )(*args)


def shards(volume, templates, wedge):
    f32, bf16 = jnp.float32, jnp.bfloat16
    count = lax.axis_size("orient")
    def swap(value, mask):
        return lax.ppermute(value, "orient", [(i, i ^ mask) for i in range(count)])

    right, small = (jnp.asarray(t) for t in filter_tables())
    normed, window = call(
        front_kernel,
        (pltpu.VMEM((TS, TS * TS), f32), pltpu.VMEM((NF, SLAB, NY), f32)),
        [
            pltpu.VMEM((TS, TS, TS), f32),
            pltpu.VMEM((TS, TS, TS), jnp.int32),
            pltpu.VMEM(right.shape, bf16),
            pltpu.VMEM(small.shape, f32),
            pltpu.VMEM((NY // LANES, SLAB, NF, LANES), f32),
            pltpu.SemaphoreType.DMA((12,)),
        ],
        (templates[0], wedge, volume, right, small), [HBM] * 5, 1 << 22, 1 << 20, None,
    )
    other = swap(normed, 6)
    fan = call(
        fan_kernel, pltpu.VMEM((8, 2 * TS, TS * TS), f32), [], (normed, other), [VMEM] * 2, 1 << 33, 1 << 18
    )
    near = [[8 * a + b for a in range(8)] for b in range(8)]
    gathered = lax.all_to_all(
        fan, "orient", 0, 0, tiled=True, axis_index_groups=near
    ).reshape(NO * TS, TS * TS)

    slabs = lax.axis_size("zslab")
    inside = lax.ppermute(window, "zslab", [(s, s ^ 1) for s in range(slabs)])
    later, inside = lax.optimization_barrier((window, inside))
    across = lax.ppermute(later, "zslab", [(1, 2), (2, 1)])
    inside, gathered = lax.optimization_barrier((inside, gathered))
    spectrum = jax.ShapeDtypeStruct((NK, 128, NY), bf16)
    high, low = call(
        volume_kernel, (spectrum, spectrum), [pltpu.VMEM((NK, 48, NY), f32)],
        (inside, window, across), [VMEM] * 3, 1 << 24, 1 << 21,
    )
    spread = jnp.asarray(spread_table(), bf16)
    strip = jax.ShapeDtypeStruct((STRIP, SLAB, NY), f32)
    parts = call(
        score_kernel, (strip,) * 4,
        [
            pltpu.VMEM((KDIM // 2 // LANES, NO * TS, LANES), f32),
            pltpu.VMEM((NK, 2, 2, NO, KDIM // 2), bf16),
            pltpu.VMEM((512, KDIM), bf16),
            pltpu.VMEM((512, KDIM), bf16),
            pltpu.VMEM((KDIM, NY), bf16),
            pltpu.VMEM((KDIM, NY), bf16),
            pltpu.VMEM((KDIM, NY), bf16),
            pltpu.VMEM((KDIM, NY), bf16),
            pltpu.VMEM((4, 256, NY), f32),
            pltpu.VMEM((4, 256, NY), f32),
            pltpu.VMEM((4, 4, 2, 128, NY), f32),
            pltpu.VMEM((NF // 2, SLAB, NY), f32),
        ],
        (gathered, spread, high, low), [VMEM] * 4, 1 << 33, 1 << 21,
    )
    late, _ = lax.optimization_barrier((inside, parts[1]))
    scale = call(
        scale_kernel, strip, [], (late, window, across), [VMEM] * 3, 1 << 22, 1 << 20
    )
    arrived = [parts[0]] + [swap(parts[m], m) for m in range(1, GROUP)]
    return call(
        last_kernel, jax.ShapeDtypeStruct((SLAB, STRIP, NY), f32), [],
        (scale, *arrived), [VMEM] * 5, 1 << 16, 1 << 18,
    )


def solution(mesh):
    return jax.shard_map(
        shards,
        mesh=mesh,
        in_specs=(P("zslab", None, None), P("orient", None, None, None), P()),
        out_specs=P("zslab", "orient", None),
        check_vma=False,
    )
```

```python
import math

import jax
import jax.numpy as jnp
import numpy as np
from jax import lax
from jax.experimental import pallas as pl
from jax.experimental.pallas import tpu as pltpu
from jax.sharding import PartitionSpec as P

TS = 16
HALF = 8
NF = 32
NK = 16
SLAB = 8
NY = 256
GROUP = 4
NO = 16
STRIP = 4
LANES = 128
KDIM = TS * 48
VMEM = pl.BlockSpec(memory_space=pltpu.VMEM)
HBM = pl.BlockSpec(memory_space=pltpu.HBM)


def plus(a, b):
    if a is None:
        return b
    return a if b is None else a + b


def minus(a, b):
    if b is None:
        return a
    return -b if a is None else a - b


def twiddled(value, k, count, sign):
    re, im = value
    if k == 0:
        return value
    if 4 * k == count:
        return (None if im is None else -sign * im, None if re is None else sign * re)
    c = math.cos(2.0 * math.pi * k / count)
    s = sign * math.sin(2.0 * math.pi * k / count)
    if im is None:
        return (c * re, s * re)
    if re is None:
        return (-s * im, c * im)
    return (c * re - s * im, s * re + c * im)


def forward(rows):
    count = len(rows)
    if count == 2:
        return [(plus(rows[0], rows[1]), None), (minus(rows[0], rows[1]), None)]
    even, odd = forward(rows[::2]), forward(rows[1::2])
    bins = [None] * (count // 2 + 1)
    for k in range(count // 4 + 1):
        e, o = even[k], twiddled(odd[k], k, count, -1.0)
        bins[k] = (plus(e[0], o[0]), plus(e[1], o[1]))
        if 4 * k != count:
            re, im = minus(e[0], o[0]), minus(e[1], o[1])
            bins[count // 2 - k] = (re, None if im is None else -im)
    return bins


def inverse_step(bins, count):
    even, odd = {}, {}
    for k in range(count // 4 + 1):
        if k not in bins:
            continue
        a, b = bins[k], bins[count // 2 - k]
        if k == 0:
            even[k] = (a[0] + b[0], None)
            odd[k] = (a[0] - b[0], None)
        elif 4 * k == count:
            even[k] = (2.0 * a[0], None)
            odd[k] = (-2.0 * a[1], None)
        else:
            even[k] = (a[0] + b[0], a[1] - b[1])
            odd[k] = twiddled((a[0] - b[0], a[1] + b[1]), k, count, 1.0)
    return even, odd


def inverse(bins, count, need):
    if count == 2:
        first = bins[0][0] + bins[1][0]
        return [first] if need == 1 else [first, bins[0][0] - bins[1][0]]
    even, odd = inverse_step(bins, count)
    rows = [None] * need
    rows[::2] = inverse(even, count // 2, (need + 1) // 2)
    rows[1::2] = inverse(odd, count // 2, need // 2)
    return rows


def slots(bins):
    return [(bins[0][0], bins[NK][0])] + [bins[k] for k in range(1, NK)]


QUADS = ((0, 4, 8, 12), (1, 7, 9, 15), (2, 6, 10, 14), (3, 5, 11, 13))


def halves(value):
    high = value.astype(jnp.bfloat16)
    return high, (value - high.astype(jnp.float32)).astype(jnp.bfloat16)


def two_terms(table):
    high = np.asarray(table, jnp.bfloat16)
    return np.stack([high, np.asarray(table - high.astype(np.float64), jnp.bfloat16)])


def filter_tables():
    small = np.arange(TS)
    pair = 2.0 * math.pi * np.outer(small, small) / TS
    two = pair[:, None, :, None] + pair[None, :, None, :]
    two = two.reshape(TS * TS, TS * TS)
    right = np.concatenate([np.cos(two), -np.sin(two)], axis=1)
    c, s = np.cos(pair), np.sin(pair)
    ahead = np.block([[c, s], [-s, c]])
    back = np.block([[c, -s], [s, c]])
    return two_terms(right), two_terms(np.stack([ahead, back]))


def spread_table():
    out = np.zeros((TS, TS, TS, 24), np.float32)
    for b in range(TS):
        for c in range(TS):
            out[c, b, b, c] = 1.0
    return out.reshape(TS * TS, KDIM // 2)


def front_kernel(
    template_hbm, wedge_hbm, volume_hbm, right_hbm, small_hbm, out_ref, window_ref,
    template_ref, wedge_ref, right_ref, small_ref, piece_ref, sems,
):
    width = TS * TS
    copies = [
        pltpu.make_async_copy(src, dst, sems.at[i])
        for i, (src, dst) in enumerate(
            ((template_hbm, template_ref), (right_hbm, right_ref), (small_hbm, small_ref), (wedge_hbm, wedge_ref))
        )
    ]
    for copy in copies:
        copy.start()
    rows = volume_hbm.shape[1]
    first = lax.axis_index("orient") // GROUP * 16 + (rows - HALF)
    pieces = []
    for j in range(NF // 8):
        at = pl.multiple_of(lax.rem(first + 8 * j, rows), 8)
        for h in range(NY // LANES):
            copy = pltpu.make_async_copy(
                volume_hbm.at[:, pl.ds(at, 8), pl.ds(h * LANES, LANES)],
                piece_ref.at[h, :, pl.ds(8 * j, 8), :],
                sems.at[4 + len(pieces)],
            )
            copy.start()
            pieces.append(copy)

    def flat(ref):
        return jnp.concatenate([ref[c].astype(jnp.float32) for c in range(TS)], axis=1)

    def across_rows(i, value):
        rows = value.shape[0]
        high, low = halves(value)
        table = jnp.concatenate([small_ref[0, i], small_ref[1, i]], axis=0)
        out = jnp.dot(table, high, preferred_element_type=jnp.float32)
        return out[:rows] + (
            out[rows:] + jnp.dot(small_ref[0, i], low, preferred_element_type=jnp.float32)
        )

    def product(value, lanes):
        rows = value.shape[0]
        both = jnp.concatenate(halves(value), axis=0)
        out = jnp.dot(both, right_ref[0, :, lanes], preferred_element_type=jnp.float32)
        low = jnp.dot(both[:rows], right_ref[1, :, lanes], preferred_element_type=jnp.float32)
        return out[:rows] + (out[rows:] + low)

    for copy in copies[:2]:
        copy.wait()
    spec = product(flat(template_ref), slice(0, 2 * width))
    spec = jnp.concatenate([spec[:, :width], spec[:, width:]], axis=0)
    for copy in copies[2:]:
        copy.wait()
    keep = flat(wedge_ref)
    spec = across_rows(0, spec) * jnp.concatenate([keep, keep], axis=0)
    spec = across_rows(1, spec)
    filt = product(spec[:TS], slice(0, width)) + product(spec[TS:], slice(width, 2 * width))
    filt = filt * (1.0 / float(TS**3))
    centered = filt - jnp.sum(filt) * (1.0 / float(TS**3))
    out_ref[...] = centered / jnp.sqrt(jnp.sum(centered * centered) + 1e-05)
    for copy in pieces:
        copy.wait()
    flat_piece = piece_ref.reshape(NY // LANES, SLAB * NF, LANES)
    for h in range(NY // LANES):
        for x in range(NF):
            window_ref[x, :, h * LANES : (h + 1) * LANES] = flat_piece[h, pl.ds(x, SLAB, stride=NF), :]


def fan_kernel(own_ref, other_ref, out_ref):
    own, other = own_ref[...], other_ref[...]
    for i in range(out_ref.shape[0]):
        out_ref[i, :TS], out_ref[i, TS:] = own, other


def volume_kernel(inside_ref, own_ref, across_ref, high_ref, low_ref, spec_ref):
    even = lax.rem(lax.axis_index("zslab"), 2) == 0
    inside_at = pl.multiple_of(jnp.where(even, 16, 0), 8)
    across_at = pl.multiple_of(16 - inside_at, 8)
    for ref, start in ((inside_ref, inside_at), (own_ref, 8), (across_ref, across_at)):
        for lane in range(0, NY, LANES):
            bins = forward([ref[x, :, lane : lane + LANES] for x in range(NF)])
            for k, (re, im) in enumerate(slots(bins)):
                spec_ref[k, pl.ds(start, 8), lane : lane + LANES] = re
                spec_ref[k, pl.ds(start + 24, 8), lane : lane + LANES] = im

    def split(k, carry):
        nil = jnp.zeros((8, NY), jnp.float32)
        for part in range(2):
            a, b, c = (spec_ref[k, 24 * part + 8 * j : 24 * part + 8 * j + 8, :] for j in range(3))
            rows = slice(64 * part, 64 * part + 64)
            high_ref[k, rows], low_ref[k, rows] = halves(
                jnp.concatenate([a, b, c, nil, nil, a, b, c], axis=0)
            )
        return carry

    lax.fori_loop(0, NK, split, 0, unroll=4)


def scale_kernel(inside_ref, own_ref, across_ref, scale_ref):
    even = lax.rem(lax.axis_index("zslab"), 2) == 0
    first = lax.rem(lax.axis_index("orient"), GROUP) * STRIP
    sums = []
    for x in range(STRIP + TS - 1):
        inside, across = inside_ref[first + x], across_ref[first + x]
        layers = jnp.concatenate(
            [jnp.where(even, across, inside), own_ref[first + x], jnp.where(even, inside, across)], axis=0
        )
        sums.append(layers * layers)
    for step in (1, 2, 4, 8):
        sums = [sums[i] + sums[i + step] for i in range(len(sums) - step)]
    for x in range(STRIP):
        total = sums[x]
        for step in (1, 2, 4, 8):
            total = total + pltpu.roll(total, 24 - step, axis=0)
        total = total[:SLAB]
        for step in (1, 2, 4, 8):
            total = total + pltpu.roll(total, NY - step, axis=1)
        total = pltpu.roll(total, HALF, axis=1)
        scale_ref[x] = (1.0 / NF) / jnp.sqrt(total * (1.0 / float(TS**3)) + 1e-05)


def score_kernel(
    gathered_ref, spread_ref, high_ref, low_ref,
    out0_ref, out1_ref, out2_ref, out3_ref,
    wide_ref, base_ref, left_a, left_b, high_a, high_b, low_a, low_b, prod_a, prod_b, part_ref, best_ref,
):
    side = KDIM // 2
    high, low = halves(gathered_ref[...])
    wide = jnp.dot(high, spread_ref[...], preferred_element_type=jnp.float32) + jnp.dot(
        low, spread_ref[...], preferred_element_type=jnp.float32
    )
    for j in range(side // LANES):
        wide_ref[j] = wide[:, j * LANES : (j + 1) * LANES]
    for j in range(side // LANES):
        groups = []
        for o in (0, 8):
            rows = [wide_ref[j, pl.ds(o * TS + a, 8, stride=TS), :] for a in range(TS)]
            groups.append(slots(forward(rows + [None] * (NF - TS))))
        for k, ((re0, im0), (re1, im1)) in enumerate(zip(*groups)):
            re = halves(jnp.concatenate([re0, re1], axis=0))
            im = halves(jnp.concatenate([im0, im1], axis=0))
            for h in range(2):
                base_ref[k, h, 0, :, j * LANES : (j + 1) * LANES] = re[h]
                base_ref[k, h, 1, :, j * LANES : (j + 1) * LANES] = im[h]

    def turned(value, shift, axis=1):
        shift = shift % value.shape[axis]
        return value if shift == 0 else pltpu.roll(value, shift, axis=axis)

    def build(k, left, right_high, right_low):
        for h in range(2):
            re, im = base_ref[k, h, 0], base_ref[k, h, 1]
            for z in range(SLAB):
                row = h * 256 + z * NO
                rows, more = slice(row, row + NO), slice(row + 128, row + 128 + NO)
                re_z, im_z = turned(re, z), turned(im, z)
                left[rows, :side] = re_z
                if k == 0:
                    nil = jnp.zeros_like(re_z)
                    left[rows, side:] = nil
                    left[more, :side] = nil
                    left[more, side:] = im_z
                else:
                    left[rows, side:] = im_z
                    left[more, :side] = -im_z
                    left[more, side:] = re_z
        for src, dst in ((high_ref, right_high), (low_ref, right_low)):
            for part in range(2):
                a, b, c, d = (src[k, 64 * part + 16 * j : 64 * part + 16 * j + 16, :] for j in range(4))
                for y in range(0, TS, 2):
                    row = side * part + 24 * y
                    here, after = HALF - y, HALF - y - 1
                    dst[row : row + 16, :] = turned(a, here)
                    dst[row + 16 : row + 32, :] = turned(b, here) + turned(c, after)
                    dst[row + 32 : row + 48, :] = turned(d, after)

    def multiply(prod, left, right_high, right_low):
        both = jnp.dot(left[...], right_high[...], preferred_element_type=jnp.float32)
        low = jnp.dot(left[:256], right_low[...], preferred_element_type=jnp.float32)
        prod[...] = both[:256] + (both[256:] + low)

    def combine(quad, prod, groups):
        for group in groups:
            row, lane = group // 2 * 8, group % 2 * LANES
            bins = {}
            for j, k in enumerate(QUADS[quad]):
                re, im = (prod[j, r : r + 8, lane : lane + LANES] for r in (row, 128 + row))
                if k == 0:
                    bins[0], bins[NK] = (re, None), (im, None)
                else:
                    bins[k] = (re, im)
            for i, one in enumerate(inverse_step(bins, NF)):
                for j, two in enumerate(inverse_step(one, NF // 2)):
                    pair = (two[0][0], two[4][0]) if quad == 0 else two[quad]
                    for part in range(2):
                        part_ref[quad, i + 2 * j, part, row : row + 8, lane : lane + LANES] = pair[part]

    order = [k for quad in QUADS for k in quad]
    slot = ((left_a, high_a, low_a), (left_b, high_b, low_b))
    prods = (prod_a, prod_b)
    build(order[0], *slot[0])
    for i in range(NK):
        multiply(prods[i // 4 % 2].at[i % 4], *slot[i % 2])
        if i + 1 < NK:
            build(order[i + 1], *slot[(i + 1) % 2])
        if i >= 4:
            combine(i // 4 - 1, prods[(i // 4 - 1) % 2], range(8 * (i % 4), 8 * (i % 4) + 8))
    combine(3, prods[1], range(32))
    best_ref[...] = jnp.zeros_like(best_ref)

    def finish(z, carry):
        row = pl.multiple_of(z * NO, NO)
        here = lax.broadcasted_iota(jnp.int32, (SLAB, LANES), 0) == z
        for lane in range(0, NY, LANES):
            for sub in range(4):
                top = None
                for o in (0, 8):
                    pairs = [
                        tuple(part_ref[q, sub, p, pl.ds(row + o, 8), lane : lane + LANES] for p in range(2))
                        for q in range(4)
                    ]
                    bins = {0: (pairs[0][0], None), 4: (pairs[0][1], None)}
                    bins.update({q: pairs[q] for q in range(1, 4)})
                    rows = inverse(bins, 8, 4)
                    top = rows if top is None else [jnp.maximum(a, b) for a, b in zip(top, rows)]
                for m in range(4):
                    x = 4 * m + sub
                    largest = jnp.max(top[m], axis=0, keepdims=True)
                    best_ref[x, :, lane : lane + LANES] = jnp.where(
                        here, largest, best_ref[x, :, lane : lane + LANES]
                    )
        return carry

    lax.fori_loop(0, SLAB, finish, 0, unroll=2)
    mine = lax.rem(lax.axis_index("orient"), GROUP)
    for m, ref in enumerate((out0_ref, out1_ref, out2_ref, out3_ref)):
        ref[...] = best_ref[pl.ds((mine ^ m) * STRIP, STRIP)]


def last_kernel(scale_ref, a_ref, b_ref, c_ref, d_ref, out_ref):
    for x in range(STRIP):
        top = jnp.maximum(jnp.maximum(a_ref[x], b_ref[x]), jnp.maximum(c_ref[x], d_ref[x]))
        out_ref[:, x, :] = top * scale_ref[x]


def call(kernel, outs, scratch, args, specs, flops=0, nbytes=0, limit=48 * 1024 * 1024):
    return pl.pallas_call(
        kernel,
        out_shape=outs,
        in_specs=specs,
        out_specs=[VMEM] * len(outs) if isinstance(outs, (list, tuple)) else VMEM,
        scratch_shapes=scratch,
        compiler_params=pltpu.CompilerParams(vmem_limit_bytes=limit),
        cost_estimate=pl.CostEstimate(flops=flops, bytes_accessed=nbytes, transcendentals=0),
    )(*args)


def shards(volume, templates, wedge):
    f32, bf16 = jnp.float32, jnp.bfloat16
    count = lax.axis_size("orient")
    def swap(value, mask):
        return lax.ppermute(value, "orient", [(i, i ^ mask) for i in range(count)])

    right, small = (jnp.asarray(t) for t in filter_tables())
    normed, window = call(
        front_kernel,
        (pltpu.VMEM((TS, TS * TS), f32), pltpu.VMEM((NF, SLAB, NY), f32)),
        [
            pltpu.VMEM((TS, TS, TS), f32),
            pltpu.VMEM((TS, TS, TS), jnp.int32),
            pltpu.VMEM(right.shape, bf16),
            pltpu.VMEM(small.shape, bf16),
            pltpu.VMEM((NY // LANES, SLAB, NF, LANES), f32),
            pltpu.SemaphoreType.DMA((12,)),
        ],
        (templates[0], wedge, volume, right, small), [HBM] * 5, 1 << 22, 1 << 20, None,
    )
    other = swap(normed, 6)
    fan = call(
        fan_kernel, pltpu.VMEM((8, 2 * TS, TS * TS), f32), [], (normed, other), [VMEM] * 2, 1 << 33, 1 << 18
    )
    near = [[8 * a + b for a in range(8)] for b in range(8)]
    gathered = lax.all_to_all(
        fan, "orient", 0, 0, tiled=True, axis_index_groups=near
    ).reshape(NO * TS, TS * TS)

    slabs = lax.axis_size("zslab")
    inside = lax.ppermute(window, "zslab", [(s, s ^ 1) for s in range(slabs)])
    later, inside = lax.optimization_barrier((window, inside))
    across = lax.ppermute(later, "zslab", [(1, 2), (2, 1)])
    inside, gathered = lax.optimization_barrier((inside, gathered))
    spectrum = jax.ShapeDtypeStruct((NK, 128, NY), bf16)
    high, low = call(
        volume_kernel, (spectrum, spectrum), [pltpu.VMEM((NK, 48, NY), f32)],
        (inside, window, across), [VMEM] * 3, 1 << 24, 1 << 21,
    )
    spread = jnp.asarray(spread_table(), bf16)
    strip = jax.ShapeDtypeStruct((STRIP, SLAB, NY), f32)
    parts = call(
        score_kernel, (strip,) * 4,
        [
            pltpu.VMEM((KDIM // 2 // LANES, NO * TS, LANES), f32),
            pltpu.VMEM((NK, 2, 2, NO, KDIM // 2), bf16),
            pltpu.VMEM((512, KDIM), bf16),
            pltpu.VMEM((512, KDIM), bf16),
            pltpu.VMEM((KDIM, NY), bf16),
            pltpu.VMEM((KDIM, NY), bf16),
            pltpu.VMEM((KDIM, NY), bf16),
            pltpu.VMEM((KDIM, NY), bf16),
            pltpu.VMEM((4, 256, NY), f32),
            pltpu.VMEM((4, 256, NY), f32),
            pltpu.VMEM((4, 4, 2, 128, NY), f32),
            pltpu.VMEM((NF // 2, SLAB, NY), f32),
        ],
        (gathered, spread, high, low), [VMEM] * 4, 1 << 33, 1 << 21,
    )
    late, _ = lax.optimization_barrier((inside, parts[1]))
    scale = call(
        scale_kernel, strip, [], (late, window, across), [VMEM] * 3, 1 << 22, 1 << 20
    )
    arrived = [parts[0]] + [swap(parts[m], m) for m in range(1, GROUP)]
    return call(
        last_kernel, jax.ShapeDtypeStruct((SLAB, STRIP, NY), f32), [],
        (scale, *arrived), [VMEM] * 5, 1 << 16, 1 << 18,
    )


def solution(mesh):
    return jax.shard_map(
        shards,
        mesh=mesh,
        in_specs=(P("zslab", None, None), P("orient", None, None, None), P()),
        out_specs=P("zslab", "orient", None),
        check_vma=False,
    )
```
